32 devices in a mesh: slide: 8 (over z, core), tile: 4 (over y, x).
Axes of the slice: x: 2, y: 2, z: 4, core: 2. Of those that a mesh axis runs over, the one named last changes fastest.
Arguments:
- features: bfloat16 [8, 4, 32, 32, 768], P('slide', 'tile'), may hold values from -6 to 6
- cotangent: bfloat16 [8, 4, 32, 32, 768], P('slide', 'tile'), may hold values from -0.59765625 to 0.59765625
- neighbours: int32 [8, 4, 8], P('slide'), may hold values from 0 to 4, as said below
- skip_flags: int32 [1, 8], P(None, 'slide'), may hold values 0 or 1
- dw_weight: float32 [1, 7, 7, 768], replicated, may hold values from -0.875 to 0.875
- ln_gain: float32 [1, 768], replicated, may hold values from 0.5 to 1.5
- ln_bias: float32 [1, 768], replicated, may hold values from -3 to 3
- up_weight: bfloat16 [1, 3072, 768], replicated, may hold values from -0.21875 to 0.21875
- up_bias: float32 [1, 3072], replicated, may hold values from -3 to 3
- down_weight: bfloat16 [1, 768, 3072], replicated, may hold values from -0.109375 to 0.109375
- down_bias: float32 [1, 768], replicated, may hold values from -3 to 3
- layer_scale: float32 [1, 768], replicated, may hold values from 0.5 to 1.5
Outputs:
- block_out: bfloat16 [8, 4, 32, 32, 768], P('slide', 'tile')
- input_grad: bfloat16 [8, 4, 32, 32, 768], P('slide', 'tile')
- weight_grads: float32 [1, 3072, 1536], P(None, ('slide', 'tile'))
- kernel_grads: float32 [1, 7, 7, 768], replicated
- channel_grads: float32 [1, 4, 768], replicated
- bias_grads: float32 [1, 3072], replicated
The draws below stay inside these ranges and needn't reach their ends.
Inputs may be any that keep to these rules, and one draw needn't show every extreme that they name: neighbours[s, a, d] is the tile of slide s next to tile a in direction d, or 4 where no tissue tile lies there; tiles of a slide sit on a grid four tiles wide, and b is a's neighbour in one direction exactly when a is b's in the opposite direction.
All inputs are finite; a program needn't handle non-finite values. No bound on the sum of `skip_flags` on one device may be relied on, other than what follows from the above.
Results may differ from the reference program's by a relative error of at most 0.015.
Values may be sent and summed in bfloat16 or wider, within the bound.
A program may use at most 192 MiB of HBM per device.

```python
import jax
import jax.numpy as jnp
from jax import lax

C = 768
HID = 3072
SIDE = 32
BLOCKS = 1
TILES = 4
SLIDES = 8


def draw_neighbours(key, part):
    step_rows = jnp.array([-1, 1, 0, 0, -1, -1, 1, 1], jnp.int32)
    step_columns = jnp.array([0, 0, -1, 1, -1, 1, -1, 1], jnp.int32)
    positions = jnp.arange(TILES, dtype=jnp.int32)

    def one_slide(slide_key):
        cells = jax.random.permutation(slide_key, 2 * TILES)[:TILES].astype(jnp.int32)
        grid_row = cells // 4
        grid_column = cells % 4
        wanted_row = grid_row[:, None] + step_rows[None, :]
        wanted_column = grid_column[:, None] + step_columns[None, :]
        matches = ((grid_row[None, None, :] == wanted_row[:, :, None]) & (grid_column[None, None, :] == wanted_column[:, :, None])).astype(jnp.int32)
        found = jnp.sum(matches, axis=2)
        which = jnp.sum(matches * positions[None, None, :], axis=2)
        return jnp.where(found > 0, which, TILES).astype(jnp.int32)
    slide_keys = jax.random.split(jax.random.fold_in(key, 7), SLIDES)
    return jax.vmap(one_slide)(slide_keys)


def place_ends(result, own_key, low, top_value):
    longest = result.shape.index(max(result.shape))
    spots = []
    for shift in (0, 1):
        where = [jax.random.randint(jax.random.fold_in(own_key, axis), (), 0, length) for axis, length in enumerate(result.shape)]
        where[longest] = (where[longest] + shift) % result.shape[longest]
        spots.append(tuple(where))
    return result.at[spots[0]].set(low).at[spots[1]].set(top_value)


def block_scale(stream_key, shape, pieces, least, top_value):
    level = 1.0
    for axis_at, blocks in pieces:
        steps = jax.random.uniform(jax.random.fold_in(jax.random.fold_in(stream_key, 6), axis_at), (blocks,), jnp.float32, least / len(pieces), top_value / len(pieces))
        level = level * jnp.repeat(jnp.exp(steps), shape[axis_at] // blocks).reshape((-1,) + (1,) * (len(shape) - 1 - axis_at))
    return level


def normal_values(key, shape, width, reach, cuts=(), held_as=jnp.bfloat16):
    values = width * jax.random.normal(key, shape, jnp.float32)
    if cuts:
        values = values * block_scale(key, shape, cuts, -0.22, 0.18)
    return jnp.clip(values, -reach, reach).astype(held_as)


def setup_inputs(seed: int = 0) -> dict:
    seeds = jax.random.split(jax.random.key(seed), 13)
    features = normal_values(seeds[0], (SLIDES, TILES, SIDE, SIDE, C), 1.0, 6.0, ((0, 8), (1, 4)))
    cotangent = normal_values(seeds[1], (SLIDES, TILES, SIDE, SIDE, C), 0.1, 0.59765625, ((0, 8), (1, 4)))
    neighbours = draw_neighbours(jax.random.fold_in(seeds[12], 71), 0)
    skip_flags = place_ends((jax.random.randint(seeds[3], (BLOCKS, SLIDES), 0, 4) < 1).astype(jnp.int32), jax.random.fold_in(seeds[3], 1), 0, 1)
    dw_weight = normal_values(seeds[4], (BLOCKS, 7, 7, C), 49 ** -0.5, 0.875, (), jnp.float32)
    ln_gain = jnp.clip(1.0 + 0.1 * jax.random.normal(seeds[5], (BLOCKS, C), jnp.float32), 0.5, 1.5)
    ln_bias = normal_values(seeds[6], (BLOCKS, C), 0.5, 3.0, (), jnp.float32)
    up_weight = normal_values(seeds[7], (BLOCKS, HID, C), C ** -0.5, 0.21875)
    up_bias = normal_values(seeds[8], (BLOCKS, HID), 0.5, 3.0, (), jnp.float32)
    down_weight = normal_values(seeds[9], (BLOCKS, C, HID), HID ** -0.5, 0.109375)
    down_bias = normal_values(seeds[10], (BLOCKS, C), 0.5, 3.0, (), jnp.float32)
    layer_scale = jnp.clip(jax.random.uniform(seeds[11], (BLOCKS, C), jnp.float32, 0.5, 1.5), 0.5, 1.5)
    return {"features": features, "cotangent": cotangent, "neighbours": neighbours, "skip_flags": skip_flags, "dw_weight": dw_weight, "ln_gain": ln_gain, "ln_bias": ln_bias, "up_weight": up_weight, "up_bias": up_bias, "down_weight": down_weight, "down_bias": down_bias, "layer_scale": layer_scale}


ln_eps = 1e-06
root_half = 0.7071067811865476
inv_root_two_pi = 0.3989422804014327
conv_dims = ('NHWC', 'HWIO', 'NHWC')

def assemble(tiles, table):
    padded = jnp.concatenate([tiles, jnp.zeros_like(tiles[:1])], 0)
    nearby = padded[table]
    upper = jnp.concatenate([nearby[:, 4, -3:, -3:], nearby[:, 0, -3:, :], nearby[:, 5, -3:, :3]], 2)
    middle = jnp.concatenate([nearby[:, 2, :, -3:], tiles, nearby[:, 3, :, :3]], 2)
    lower = jnp.concatenate([nearby[:, 6, :3, -3:], nearby[:, 1, :3, :], nearby[:, 7, :3, :3]], 2)
    return jnp.concatenate([upper, middle, lower], 1)

def depthwise(extended, kernel):
    channels = kernel.shape[-1]
    return lax.conv_general_dilated(extended, kernel[:, :, None, :], (1, 1), 'VALID', dimension_numbers=conv_dims, feature_group_count=channels, precision=lax.Precision.HIGHEST)

def kernel_grad(extended, conv_grad):
    channels = conv_grad.shape[-1]
    total = jnp.zeros((7, 7, channels), jnp.float32)
    for tile_pos in range(conv_grad.shape[0]):
        kernel = jnp.transpose(conv_grad[tile_pos:tile_pos + 1], (1, 2, 0, 3))
        single = lax.conv_general_dilated(extended[tile_pos:tile_pos + 1], kernel, (1, 1), 'VALID', dimension_numbers=conv_dims, feature_group_count=channels, precision=lax.Precision.HIGHEST)
        total = total + single[0]
    return total

def normalize(values):
    average = lax.optimization_barrier(jnp.mean(values, axis=-1, keepdims=True))
    centred = values - average
    inv_std = lax.rsqrt(lax.optimization_barrier(jnp.mean(centred * centred, axis=-1, keepdims=True)) + ln_eps)
    return (centred * inv_std, inv_std)

def gelu_parts(pre):
    cdf = 0.5 * (1.0 + lax.erf(pre * root_half))
    return (cdf, cdf + pre * inv_root_two_pi * jnp.exp(-0.5 * pre * pre))

def contract(left, right):
    return lax.dot_general(left, right, (((1,), (1,)), ((), ())), preferred_element_type=jnp.float32)

def over_pixels(left, right):
    return lax.dot_general(left, right, (((0,), (0,)), ((), ())), preferred_element_type=jnp.float32)

def reference(features, cotangent, neighbours, skip_flags, dw_weight, ln_gain, ln_bias, up_weight, up_bias, down_weight, down_bias, layer_scale):
    blocks = dw_weight.shape[0]
    channels = features.shape[-1]
    hidden_units = up_weight.shape[1]
    tile_shape = features.shape[1:]

    def one_slide(totals, slide_data):
        tiles, tile_grad, table, skips = slide_data
        current = tiles
        saved = []
        for layer in range(blocks):
            keep = (1 - skips[layer]).astype(jnp.float32)
            extended = assemble(current, table).astype(jnp.float32)
            conv = depthwise(extended, dw_weight[layer])
            whitened, inv_std = normalize(conv.reshape(-1, channels))
            flat = (whitened * ln_gain[layer] + ln_bias[layer]).astype(jnp.bfloat16)
            pre = contract(flat, up_weight[layer]) + up_bias[layer]
            cdf, slope = gelu_parts(pre)
            act = (pre * cdf).astype(jnp.bfloat16)
            branch = contract(act, down_weight[layer]) + down_bias[layer]
            output = (current.astype(jnp.float32).reshape(-1, channels) + keep * layer_scale[layer] * branch).astype(jnp.bfloat16)
            saved.append((extended, whitened, inv_std, flat, pre, act, branch, keep))
            current = output.reshape(tile_shape)
        weight_total, kernel_total, channel_total, bias_total = totals
        step_grad = tile_grad
        for layer in reversed(range(blocks)):
            extended, whitened, inv_std, flat, pre, act, branch, keep = saved[layer]
            grad_flat = step_grad.astype(jnp.float32).reshape(-1, channels)
            scale_grad = lax.optimization_barrier(jnp.sum(grad_flat * keep * branch, axis=0))
            branch_grad = (keep * layer_scale[layer] * grad_flat).astype(jnp.bfloat16)
            act_grad = jnp.dot(branch_grad, down_weight[layer], preferred_element_type=jnp.float32)
            cdf, slope = gelu_parts(pre)
            pre_grad = (act_grad * slope).astype(jnp.bfloat16)
            normed_grad = jnp.dot(pre_grad, up_weight[layer], preferred_element_type=jnp.float32)
            scaled = normed_grad * ln_gain[layer]
            conv_grad = inv_std * (scaled - lax.optimization_barrier(jnp.mean(scaled, axis=-1, keepdims=True)) - whitened * lax.optimization_barrier(jnp.mean(scaled * whitened, axis=-1, keepdims=True)))
            conv_grad = conv_grad.astype(jnp.bfloat16).reshape(tile_shape)
            weight_term = jnp.concatenate([over_pixels(pre_grad, flat), over_pixels(act, branch_grad)], 1)
            weight_total = weight_total.at[layer].add(weight_term)
            kernel_total = kernel_total.at[layer].add(kernel_grad(extended, conv_grad.astype(jnp.float32)))
            channel_term = jnp.stack([lax.optimization_barrier(jnp.sum(normed_grad * whitened, axis=0)), lax.optimization_barrier(jnp.sum(normed_grad, axis=0)), lax.optimization_barrier(jnp.sum(branch_grad.astype(jnp.float32), axis=0)), scale_grad])
            channel_total = channel_total.at[layer].add(channel_term)
            bias_total = bias_total.at[layer].add(lax.optimization_barrier(jnp.sum(pre_grad.astype(jnp.float32), axis=0)))
            grad_extended = assemble(conv_grad, table).astype(jnp.float32)
            back = depthwise(grad_extended, dw_weight[layer][::-1, ::-1])
            step_grad = (step_grad.astype(jnp.float32) + back).astype(jnp.bfloat16)
        return ((weight_total, kernel_total, channel_total, bias_total), (current, step_grad))
    start = (jnp.zeros((blocks, hidden_units, 2 * channels), jnp.float32), jnp.zeros((blocks, 7, 7, channels), jnp.float32), jnp.zeros((blocks, 4, channels), jnp.float32), jnp.zeros((blocks, hidden_units), jnp.float32))
    totals, results = lax.scan(one_slide, start, (features, cotangent, neighbours, jnp.transpose(skip_flags)))
    block_out, input_grad = results
    weight_grads, kernel_grads, channel_grads, bias_grads = totals
    return (block_out, input_grad, weight_grads, kernel_grads, channel_grads, bias_grads)
```

```python
import functools

import jax
import jax.numpy as jnp
from jax import lax
from jax.experimental import pallas as pl
from jax.experimental.pallas import tpu as pltpu
from jax.sharding import PartitionSpec as P

ln_eps = 1e-06
root_half = 0.7071067811865476
inv_root_two_pi = 0.3989422804014327
kind_of = (0, 1, 2, 3, 0, 0, 1, 1)
lanes = 128
row_step = 4
vmem_bytes = 56 * 1024 * 1024


def params(**more):
    return pltpu.CompilerParams(vmem_limit_bytes=vmem_bytes, **more)


def exchange_rims(tile, table, me, count):
    side, _, channels = tile.shape
    columns = lambda part: jnp.transpose(part, (1, 0, 2))
    strips = jnp.stack([tile[-3:], tile[:3], columns(tile[:, -3:]), columns(tile[:, :3])])
    strips = strips.reshape(4, 3 * side, channels)
    kinds = jnp.array(kind_of, jnp.int32)
    slots = [jnp.zeros_like(strips[0])]
    for offset in range(1, count):
        peer = lax.rem(me + offset, count)
        rows = lax.dynamic_index_in_dim(table, peer, 0, keepdims=False)
        kind = jnp.sum(jnp.where(rows == me, kinds, 0))
        message = lax.dynamic_index_in_dim(strips, kind, 0, keepdims=False)
        perm = [(i, (i + offset) % count) for i in range(count)]
        slots.append(lax.ppermute(message, "tile", perm))
    slots = jnp.stack(slots).reshape(count, 3, side, channels)
    mine = lax.dynamic_index_in_dim(table, me, 0, keepdims=False)
    place = jnp.where(mine == count, 0, lax.rem(me - mine + count, count))
    strip = [lax.dynamic_index_in_dim(slots, place[d], 0, keepdims=False) for d in range(8)]
    blank = jnp.zeros((3, 5, channels), tile.dtype)

    def edge(left, centre, right):
        whole = jnp.concatenate([blank, left[:, -3:], centre, right[:, :3], blank], 1)
        return whole.astype(jnp.float32)

    top = edge(strip[4], strip[0], strip[5])
    bottom = edge(strip[6], strip[1], strip[7])
    west = jnp.pad(columns(strip[2]), ((0, 0), (5, 0), (0, 0))).astype(jnp.float32)
    east = jnp.pad(columns(strip[3]), ((0, 0), (0, 5), (0, 0))).astype(jnp.float32)
    return top, bottom, west, east


def fill(ext, tile_ref, top_ref, bottom_ref, west_ref, east_ref):
    side = tile_ref.shape[0]
    ext[0:3] = top_ref[...]
    ext[side + 3 : side + 6] = bottom_ref[...]
    ext[3 : side + 3, 0:8] = west_ref[...]
    ext[3 : side + 3, 8 : side + 8] = tile_ref[...].astype(jnp.float32)
    ext[3 : side + 3, side + 8 : side + 16] = east_ref[...]


def conv_body(with_add, tile_ref, top, bottom, west, east, weight_ref, *rest):
    if with_add:
        add_ref, out_ref, ext, shifted, total = rest
    else:
        out_ref, ext, shifted, total = rest
    side = tile_ref.shape[0]
    fill(ext, tile_ref, top, bottom, west, east)
    for b in range(7):
        if b == 3:
            source, base = ext, 8
        else:
            shifted[...] = ext[:, 5 + b : 5 + b + side]
            source, base = shifted, 0
        taps = [
            jnp.broadcast_to(weight_ref[a * 7 + b : a * 7 + b + 1, :], (8, lanes)) for a in range(7)
        ]

        def rows(step, carry, b=b, source=source, base=base, taps=taps):
            first = step * row_step
            for group in range(side // 8):
                at = pl.ds(base + group * 8, 8)
                here = pl.ds(group * 8, 8)
                sums = [None] * row_step
                for r in range(row_step + 6):
                    value = source[first + r, at]
                    for i in range(row_step):
                        a = r - i
                        if 0 <= a < 7:
                            term = value * taps[a]
                            sums[i] = term if sums[i] is None else sums[i] + term
                for i in range(row_step):
                    if b > 0:
                        sums[i] = sums[i] + total[first + i, here]
                    total[first + i, here] = sums[i]
            return carry

        lax.fori_loop(0, side // row_step, rows, 0)
    if with_add:
        out_ref[...] = (add_ref[...].astype(jnp.float32) + total[...]).astype(jnp.bfloat16)
    else:
        out_ref[...] = total[...]


def tile_spec(shape):
    return pl.BlockSpec(shape[:-1] + (lanes,), lambda c: (0,) * (len(shape) - 1) + (c,))


def depthwise(tile, rims, weight, add=None):
    side, _, channels = tile.shape
    operands = [tile, *rims, weight] + ([] if add is None else [add])
    out = jax.ShapeDtypeStruct(tile.shape, jnp.float32 if add is None else jnp.bfloat16)
    flops = 2 * 49 * side * side * channels
    return pl.pallas_call(
        functools.partial(conv_body, add is not None),
        out_shape=out,
        grid=(channels // lanes,),
        in_specs=[tile_spec(o.shape) for o in operands],
        out_specs=tile_spec(out.shape),
        scratch_shapes=[
            pltpu.VMEM((side + 6, side + 16, lanes), jnp.float32),
            pltpu.VMEM((side + 6, side, lanes), jnp.float32),
            pltpu.VMEM((side, side, lanes), jnp.float32),
        ],
        compiler_params=params(),
        cost_estimate=pl.CostEstimate(flops=100 * flops, bytes_accessed=8 << 20, transcendentals=0),
        name="depthwise",
    )(*operands)


def kernel_grad_body(tile_ref, top, bottom, west, east, grad_ref, out_ref, ext, shifted, grad):
    side = tile_ref.shape[0]
    fill(ext, tile_ref, top, bottom, west, east)
    grad[...] = grad_ref[...].astype(jnp.float32)
    for b in range(7):
        if b == 3:
            source, base = ext, 8
        else:
            shifted[...] = ext[:, 5 + b : 5 + b + side]
            source, base = shifted, 0

        def rows(step, sums, source=source, base=base):
            first = step * row_step
            sums = list(sums)
            for group in range(side // 8):
                at = pl.ds(base + group * 8, 8)
                here = pl.ds(group * 8, 8)
                near = [grad[first + i, here] for i in range(row_step)]
                for r in range(row_step + 6):
                    value = source[first + r, at]
                    for i in range(row_step):
                        a = r - i
                        if 0 <= a < 7:
                            slot = a * 2 + i % 2
                            sums[slot] = sums[slot] + value * near[i]
            return tuple(sums)

        zero = jnp.zeros((8, lanes), jnp.float32)
        sums = lax.fori_loop(0, side // row_step, rows, (zero,) * 14)
        for a in range(7):
            out_ref[a * 7 + b : a * 7 + b + 1, :] = jnp.sum(
                sums[2 * a] + sums[2 * a + 1], axis=0, keepdims=True
            )


def kernel_grad(tile, rims, conv_grad):
    side, _, channels = tile.shape
    operands = [tile, *rims, conv_grad]
    flops = 2 * 49 * side * side * channels
    return pl.pallas_call(
        kernel_grad_body,
        out_shape=jax.ShapeDtypeStruct((49, channels), jnp.float32),
        grid=(channels // lanes,),
        in_specs=[tile_spec(o.shape) for o in operands],
        out_specs=tile_spec((49, channels)),
        scratch_shapes=[
            pltpu.VMEM((side + 6, side + 16, lanes), jnp.float32),
            pltpu.VMEM((side + 6, side, lanes), jnp.float32),
            pltpu.VMEM((side, side, lanes), jnp.float32),
        ],
        compiler_params=params(),
        cost_estimate=pl.CostEstimate(flops=100 * flops, bytes_accessed=8 << 20, transcendentals=0),
        name="kernel_grad",
    )(*operands)


def nt(left, right):
    return lax.dot_general(
        left, right, (((1,), (1,)), ((), ())), preferred_element_type=jnp.float32
    )


def nn(left, right):
    return jnp.dot(left, right, preferred_element_type=jnp.float32)


def mlp_body(
    conv_ref,
    x_ref,
    g_ref,
    keep_ref,
    gain_ref,
    shift_ref,
    up_ref,
    up_bias_ref,
    down_ref,
    down_bias_ref,
    scale_ref,
    block_out_ref,
    conv_grad_ref,
    up_grad_ref,
    down_grad_ref,
    sums_ref,
    bias_ref,
    flat,
    branch_grad,
    inv,
    white,
    branch,
    normed_grad,
):
    step = pl.program_id(0)
    pixels, channels = conv_ref.shape
    part = 128

    @pl.when(step == 0)
    def _():
        keep = keep_ref[0:1, 0:1]

        def body(i, total):
            at = pl.ds(pl.multiple_of(i * part, part), part)
            values = conv_ref[at, :]
            centred = values - jnp.mean(values, axis=-1, keepdims=True)
            inv_std = lax.rsqrt(jnp.mean(centred * centred, axis=-1, keepdims=True) + ln_eps)
            whitened = centred * inv_std
            white[at, :] = whitened
            inv[at, :] = jnp.broadcast_to(inv_std, (part, lanes))
            flat[at, :] = (whitened * gain_ref[...] + shift_ref[...]).astype(jnp.bfloat16)
            own = (keep * scale_ref[...] * g_ref[at, :].astype(jnp.float32)).astype(jnp.bfloat16)
            branch_grad[at, :] = own
            return total + jnp.sum(own.astype(jnp.float32), axis=0, keepdims=True)

        zero = jnp.zeros((1, channels), jnp.float32)
        sums_ref[2:3, :] = lax.fori_loop(0, pixels // part, body, zero)
        branch[...] = jnp.zeros_like(branch)
        normed_grad[...] = jnp.zeros_like(normed_grad)

    up, down = up_ref[...], down_ref[...]
    pre = nt(flat[...], up) + up_bias_ref[...]
    act_grad = nn(branch_grad[...], down)
    cdf = 0.5 * (1.0 + lax.erf(pre * root_half))
    slope = cdf + pre * inv_root_two_pi * jnp.exp(-0.5 * pre * pre)
    act = (pre * cdf).astype(jnp.bfloat16)
    pre_grad_wide = act_grad * slope
    pre_grad = pre_grad_wide.astype(jnp.bfloat16)
    branch[...] += nt(act, down)
    normed_grad[...] += nn(pre_grad, up)
    bias_ref[...] = jnp.sum(pre_grad.astype(jnp.float32), axis=0, keepdims=True)
    up_grad_ref[...] = nn(pre_grad.T, flat[...]).astype(jnp.bfloat16)
    down_grad_ref[...] = nn(act.T, branch_grad[...]).astype(jnp.bfloat16)

    @pl.when(step == pl.num_programs(0) - 1)
    def _():
        keep = keep_ref[0:1, 0:1]

        def body(i, totals):
            at = pl.ds(pl.multiple_of(i * part, part), part)
            out = branch[at, :] + down_bias_ref[...]
            g = g_ref[at, :].astype(jnp.float32)
            block_out_ref[at, :] = (
                x_ref[at, :].astype(jnp.float32) + keep * scale_ref[...] * out
            ).astype(jnp.bfloat16)
            whitened = white[at, :]
            own = normed_grad[at, :]
            scaled = own * gain_ref[...]
            spread = whitened * jnp.mean(scaled * whitened, axis=-1, keepdims=True)
            centred = scaled - jnp.mean(scaled, axis=-1, keepdims=True) - spread
            conv_grad_ref[at, :] = (inv[at, 0:1] * centred).astype(jnp.bfloat16)
            down_sum = lambda v: jnp.sum(v, axis=0, keepdims=True)
            terms = (own * whitened, own, g * keep * out)
            return tuple(t + down_sum(v) for t, v in zip(totals, terms))

        zero = jnp.zeros((1, channels), jnp.float32)
        totals = lax.fori_loop(0, pixels // part, body, (zero,) * 3)
        sums_ref[0:1, :] = totals[0]
        sums_ref[1:2, :] = totals[1]
        sums_ref[3:4, :] = totals[2]


def mlp(conv, x, g, keep, gain, shift, up, up_bias, down, down_bias, scale):
    pixels, channels = conv.shape
    hidden = up.shape[0]
    block = 256
    whole = lambda shape: pl.BlockSpec(
        shape, lambda j: (0, 0), pipeline_mode=pl.Buffered(buffer_count=1)
    )
    full = lambda shape: pl.BlockSpec(shape, lambda j: (0, 0))
    row = pl.BlockSpec((1, channels), lambda j: (0, 0))
    return pl.pallas_call(
        mlp_body,
        out_shape=(
            jax.ShapeDtypeStruct((pixels, channels), jnp.bfloat16),
            jax.ShapeDtypeStruct((pixels, channels), jnp.bfloat16),
            jax.ShapeDtypeStruct((hidden, channels), jnp.bfloat16),
            jax.ShapeDtypeStruct((hidden, channels), jnp.bfloat16),
            jax.ShapeDtypeStruct((4, channels), jnp.float32),
            jax.ShapeDtypeStruct((1, hidden), jnp.float32),
        ),
        grid=(hidden // block,),
        in_specs=[
            whole((pixels, channels)),
            whole((pixels, channels)),
            whole((pixels, channels)),
            pl.BlockSpec((1, lanes), lambda j: (0, 0)),
            row,
            row,
            pl.BlockSpec((block, channels), lambda j: (j, 0)),
            pl.BlockSpec((1, block), lambda j: (0, j)),
            pl.BlockSpec((channels, block), lambda j: (0, j)),
            row,
            row,
        ],
        out_specs=(
            full((pixels, channels)),
            full((pixels, channels)),
            pl.BlockSpec((block, channels), lambda j: (j, 0)),
            pl.BlockSpec((block, channels), lambda j: (j, 0)),
            pl.BlockSpec((4, channels), lambda j: (0, 0)),
            pl.BlockSpec((1, block), lambda j: (0, j)),
        ),
        scratch_shapes=[
            pltpu.VMEM((pixels, channels), jnp.bfloat16),
            pltpu.VMEM((pixels, channels), jnp.bfloat16),
            pltpu.VMEM((pixels, lanes), jnp.float32),
            pltpu.VMEM((pixels, channels), jnp.float32),
            pltpu.VMEM((pixels, channels), jnp.float32),
            pltpu.VMEM((pixels, channels), jnp.float32),
        ],
        compiler_params=params(),
        cost_estimate=pl.CostEstimate(
            flops=12 * pixels * channels * hidden,
            bytes_accessed=32 << 20,
            transcendentals=2 * pixels * hidden,
        ),
        name="mlp",
    )(conv, x, g, keep, gain, shift, up, up_bias, down, down_bias, scale)


class Grid:
    def __init__(self, slides, tiles):
        self.sizes = {"rest": slides // 2, "core": 2, "hi": 2, "lo": tiles // 2}
        self.names = ("rest", "core", "hi", "lo")
        slide, tile = lax.axis_index("slide"), lax.axis_index("tile")
        self.place = {
            "rest": slide // 2,
            "core": lax.rem(slide, 2),
            "hi": tile // (tiles // 2),
            "lo": lax.rem(tile, tiles // 2),
        }

    def perm(self, axis, move):
        pairs = []
        extents = [self.sizes[n] for n in self.names]
        at = self.names.index(axis)
        stride = 1
        for size in extents[at + 1 :]:
            stride *= size
        total = 1
        for size in extents:
            total *= size
        for device in range(total):
            own = (device // stride) % extents[at]
            pairs.append((device, device + (move(own) - own) * stride))
        return pairs

    def send(self, value, axis, move):
        return lax.ppermute(value, ("slide", "tile"), self.perm(axis, move))

    def scatter(self, value, dim, axis, last=False):
        size, own = self.sizes[axis], self.place[axis]
        pick = lambda i: lax.dynamic_index_in_dim(value, i, dim, keepdims=False)
        total = pick(own).astype(jnp.float32)
        for offset in range(1, size):
            block = pick(lax.rem(own + offset, size))
            came = self.send(block, axis, lambda i, o=offset: (i + o) % size)
            total = total + came.astype(jnp.float32)
        return total if last else total.astype(jnp.bfloat16)

    def everywhere(self, value):
        for axis in self.names[::-1]:
            step = 1
            while step < self.sizes[axis]:
                value = value + self.send(value, axis, lambda i, s=step: i ^ s)
                step *= 2
        return value


def on_device(
    features,
    cotangent,
    neighbours,
    skip_flags,
    dw_weight,
    ln_gain,
    ln_bias,
    up_weight,
    up_bias,
    down_weight,
    down_bias,
    layer_scale,
):
    slides, tiles = lax.axis_size("slide"), lax.axis_size("tile")
    side, channels = features.shape[3], features.shape[4]
    hidden = up_weight.shape[1]
    me = lax.axis_index("tile")
    table = neighbours[0]
    grid = Grid(slides, tiles)
    tile, grad = features[0, 0], cotangent[0, 0]
    taps = dw_weight[0].reshape(49, channels)
    keep = jnp.broadcast_to((1 - skip_flags[0, 0]).astype(jnp.float32), (1, lanes))

    rims = exchange_rims(tile, table, me, tiles)
    conv = depthwise(tile, rims, taps)
    block_out, conv_grad, up_grad, down_grad, sums, bias = mlp(
        conv.reshape(-1, channels),
        tile.reshape(-1, channels),
        grad.reshape(-1, channels),
        keep,
        ln_gain,
        ln_bias,
        up_weight[0],
        up_bias,
        down_weight[0],
        down_bias,
        layer_scale,
    )
    conv_tile = conv_grad.reshape(side, side, channels)
    grad_rims = exchange_rims(conv_tile, table, me, tiles)

    shape = tuple(grid.sizes[n] for n in grid.names)
    up_part = grid.scatter(up_grad.reshape(*shape, -1, channels), 1, "core")
    down_part = grid.scatter(down_grad.reshape(*shape, -1, channels), 1, "core")
    up_part = grid.scatter(up_part, 1, "hi")
    down_part = grid.scatter(down_part, 2, "lo")
    up_part = grid.scatter(up_part, 1, "lo")
    down_part = grid.scatter(down_part, 1, "hi")
    up_part = grid.scatter(up_part, 0, "rest", last=True)
    down_part = grid.scatter(down_part, 0, "rest", last=True)
    weight_grads = jnp.concatenate([up_part, down_part], -1)[None]

    kernel_sum = kernel_grad(tile, rims, conv_tile)
    small = jnp.concatenate([kernel_sum, sums, bias.reshape(-1, channels)], 0)
    small = grid.everywhere(small)
    input_grad = depthwise(conv_tile, grad_rims, taps[::-1], grad)
    return (
        block_out.reshape(1, 1, side, side, channels),
        input_grad[None, None],
        weight_grads,
        small[:49].reshape(1, 7, 7, channels),
        small[49:53][None],
        small[53:].reshape(1, hidden),
    )


def solution(mesh):
    tiles = P("slide", "tile", None, None, None)
    return jax.shard_map(
        on_device,
        mesh=mesh,
        in_specs=(tiles, tiles, P("slide", None, None), P(None, "slide")) + (P(),) * 8,
        out_specs=(tiles, tiles, P(None, ("slide", "tile"), None), P(), P(), P()),
        check_vma=False,
    )
```

```python
import functools

import jax
import jax.numpy as jnp
from jax import lax
from jax.experimental import pallas as pl
from jax.experimental.pallas import tpu as pltpu
from jax.sharding import PartitionSpec as P

ln_eps = 1e-06
root_half = 0.7071067811865476
inv_root_two_pi = 0.3989422804014327
kind_of = (0, 1, 2, 3, 0, 0, 1, 1)
lanes = 128
row_step = 4
vmem_bytes = 60 * 1024 * 1024


def params(**more):
    return pltpu.CompilerParams(vmem_limit_bytes=vmem_bytes, **more)


def rim_body(
    count, table, tile, top, bottom, west, east, strips, sends, slots, send_sem, recv_sem
):
    side = tile.shape[0]
    me = lax.axis_index("tile")
    peers = [lax.rem(me + offset, count) for offset in range(1, count)]
    barrier = pltpu.get_barrier_semaphore()
    for peer in peers:
        pl.semaphore_signal(
            barrier, inc=1, device_id={"tile": peer}, device_id_type=pl.DeviceIdType.MESH
        )
    for k in range(3):
        at = pl.ds(k * side, side)
        strips[0, at] = tile[side - 3 + k].astype(jnp.float32)
        strips[1, at] = tile[k].astype(jnp.float32)
    for h in range(side):
        row = tile[h].astype(jnp.float32)
        strips[2, 3 * h : 3 * h + 3] = row[side - 3 :]
        strips[3, 3 * h : 3 * h + 3] = row[:3]
    slots[0] = jnp.zeros(slots.shape[1:], slots.dtype)
    pl.semaphore_wait(barrier, count - 1)
    copies = []
    for i, peer in enumerate(peers):
        kind = jnp.int32(0)
        for d in range(8):
            kind = jnp.where(table[peer, d] == me, kind_of[d], kind)
        sends[i] = strips[kind].astype(jnp.bfloat16)
        copy = pltpu.make_async_remote_copy(
            src_ref=sends.at[i],
            dst_ref=slots.at[i + 1],
            send_sem=send_sem.at[i],
            recv_sem=recv_sem.at[i],
            device_id={"tile": peer},
            device_id_type=pl.DeviceIdType.MESH,
        )
        copy.start()
        copies.append(copy)
    top[...] = jnp.zeros_like(top)
    bottom[...] = jnp.zeros_like(bottom)
    west[...] = jnp.zeros_like(west)
    east[...] = jnp.zeros_like(east)
    for copy in copies:
        copy.wait()

    def load(slot, d):
        other = table[me, d]
        place = jnp.where(other == count, 0, lax.rem(me - other + count, count))
        strips[slot] = slots[place].astype(jnp.float32)

    for edge, (left, centre, right) in ((top, (4, 0, 5)), (bottom, (6, 1, 7))):
        load(0, left)
        load(1, centre)
        load(2, right)
        for k in range(3):
            edge[k, 5:8] = strips[0, k * side + side - 3 : k * side + side]
            edge[k, 8 : 8 + side] = strips[1, k * side : k * side + side]
            edge[k, 8 + side : 11 + side] = strips[2, k * side : k * side + 3]
    load(0, 2)
    load(1, 3)
    for h in range(side):
        west[h, 5:8] = strips[0, 3 * h : 3 * h + 3]
        east[h, 0:3] = strips[1, 3 * h : 3 * h + 3]


def exchange_rims(tile, table, count, call):
    side, _, channels = tile.shape
    vmem = pl.BlockSpec(memory_space=pltpu.VMEM)
    edge = jax.ShapeDtypeStruct((3, side + 16, channels), jnp.float32)
    flank = jax.ShapeDtypeStruct((side, 8, channels), jnp.float32)
    return pl.pallas_call(
        functools.partial(rim_body, count),
        out_shape=(edge, edge, flank, flank),
        in_specs=[pl.BlockSpec(memory_space=pltpu.SMEM), vmem],
        out_specs=(vmem,) * 4,
        scratch_shapes=[
            pltpu.VMEM((4, 3 * side, channels), jnp.float32),
            pltpu.VMEM((count - 1, 3 * side, channels), jnp.bfloat16),
            pltpu.VMEM((count, 3 * side, channels), jnp.bfloat16),
            pltpu.SemaphoreType.DMA((count - 1,)),
            pltpu.SemaphoreType.DMA((count - 1,)),
        ],
        compiler_params=params(collective_id=call, has_side_effects=True),
        cost_estimate=pl.CostEstimate(
            flops=10**9, bytes_accessed=8 << 20, transcendentals=0
        ),
        name="rims" + str(call),
    )(table, tile)


def fill(ext, tile_ref, top_ref, bottom_ref, west_ref, east_ref):
    side = tile_ref.shape[0]
    ext[0:3] = top_ref[...]
    ext[side + 3 : side + 6] = bottom_ref[...]
    ext[3 : side + 3, 0:8] = west_ref[...]
    ext[3 : side + 3, 8 : side + 8] = tile_ref[...].astype(jnp.float32)
    ext[3 : side + 3, side + 8 : side + 16] = east_ref[...]


def conv_body(with_add, tile_ref, top, bottom, west, east, weight_ref, *rest):
    if with_add:
        add_ref, out_ref, ext, shifted, total = rest
    else:
        out_ref, ext, shifted, total = rest
    side = tile_ref.shape[0]
    fill(ext, tile_ref, top, bottom, west, east)
    for b in range(7):
        if b == 3:
            source, base = ext, 8
        else:
            shifted[...] = ext[:, 5 + b : 5 + b + side]
            source, base = shifted, 0
        taps = [
            jnp.broadcast_to(weight_ref[a * 7 + b : a * 7 + b + 1, :], (8, lanes)) for a in range(7)
        ]

        def rows(step, carry, b=b, source=source, base=base, taps=taps):
            first = step * row_step
            for group in range(side // 8):
                at = pl.ds(base + group * 8, 8)
                here = pl.ds(group * 8, 8)
                sums = [None] * row_step
                for r in range(row_step + 6):
                    value = source[first + r, at]
                    for i in range(row_step):
                        a = r - i
                        if 0 <= a < 7:
                            term = value * taps[a]
                            sums[i] = term if sums[i] is None else sums[i] + term
                for i in range(row_step):
                    if b > 0:
                        sums[i] = sums[i] + total[first + i, here]
                    total[first + i, here] = sums[i]
            return carry

        lax.fori_loop(0, side // row_step, rows, 0)
    if with_add:
        out_ref[...] = (add_ref[...].astype(jnp.float32) + total[...]).astype(jnp.bfloat16)
    else:
        out_ref[...] = total[...]


def tile_spec(shape):
    return pl.BlockSpec(shape[:-1] + (lanes,), lambda c: (0,) * (len(shape) - 1) + (c,))


def depthwise(tile, rims, weight, add=None):
    side, _, channels = tile.shape
    operands = [tile, *rims, weight] + ([] if add is None else [add])
    out = jax.ShapeDtypeStruct(tile.shape, jnp.float32 if add is None else jnp.bfloat16)
    flops = 2 * 49 * side * side * channels
    return pl.pallas_call(
        functools.partial(conv_body, add is not None),
        out_shape=out,
        grid=(channels // lanes,),
        in_specs=[tile_spec(o.shape) for o in operands],
        out_specs=tile_spec(out.shape),
        scratch_shapes=[
            pltpu.VMEM((side + 6, side + 16, lanes), jnp.float32),
            pltpu.VMEM((side + 6, side, lanes), jnp.float32),
            pltpu.VMEM((side, side, lanes), jnp.float32),
        ],
        compiler_params=params(),
        cost_estimate=pl.CostEstimate(flops=100 * flops, bytes_accessed=8 << 20, transcendentals=0),
        name="depthwise",
    )(*operands)


def kernel_grad_body(tile_ref, top, bottom, west, east, grad_ref, out_ref, ext, shifted, grad):
    side = tile_ref.shape[0]
    fill(ext, tile_ref, top, bottom, west, east)
    grad[...] = grad_ref[...].astype(jnp.float32)
    for b in range(7):
        if b == 3:
            source, base = ext, 8
        else:
            shifted[...] = ext[:, 5 + b : 5 + b + side]
            source, base = shifted, 0

        def rows(step, sums, source=source, base=base):
            first = step * row_step
            sums = list(sums)
            for group in range(side // 8):
                at = pl.ds(base + group * 8, 8)
                here = pl.ds(group * 8, 8)
                near = [grad[first + i, here] for i in range(row_step)]
                for r in range(row_step + 6):
                    value = source[first + r, at]
                    for i in range(row_step):
                        a = r - i
                        if 0 <= a < 7:
                            slot = a * 2 + i % 2
                            sums[slot] = sums[slot] + value * near[i]
            return tuple(sums)

        zero = jnp.zeros((8, lanes), jnp.float32)
        sums = lax.fori_loop(0, side // row_step, rows, (zero,) * 14)
        for a in range(7):
            out_ref[a * 7 + b : a * 7 + b + 1, :] = jnp.sum(
                sums[2 * a] + sums[2 * a + 1], axis=0, keepdims=True
            )


def kernel_grad(tile, rims, conv_grad):
    side, _, channels = tile.shape
    operands = [tile, *rims, conv_grad]
    flops = 2 * 49 * side * side * channels
    return pl.pallas_call(
        kernel_grad_body,
        out_shape=jax.ShapeDtypeStruct((49, channels), jnp.float32),
        grid=(channels // lanes,),
        in_specs=[tile_spec(o.shape) for o in operands],
        out_specs=tile_spec((49, channels)),
        scratch_shapes=[
            pltpu.VMEM((side + 6, side + 16, lanes), jnp.float32),
            pltpu.VMEM((side + 6, side, lanes), jnp.float32),
            pltpu.VMEM((side, side, lanes), jnp.float32),
        ],
        compiler_params=params(),
        cost_estimate=pl.CostEstimate(flops=100 * flops, bytes_accessed=8 << 20, transcendentals=0),
        name="kernel_grad",
    )(*operands)


def nt(left, right):
    return lax.dot_general(
        left, right, (((1,), (1,)), ((), ())), preferred_element_type=jnp.float32
    )


def nn(left, right):
    return jnp.dot(left, right, preferred_element_type=jnp.float32)


def mlp_body(
    extents,
    conv_ref,
    x_ref,
    g_ref,
    keep_ref,
    gain_ref,
    shift_ref,
    up_ref,
    up_bias_ref,
    down_ref,
    down_bias_ref,
    scale_ref,
    block_out_ref,
    conv_grad_ref,
    up_grad_ref,
    down_grad_ref,
    sums_ref,
    bias_ref,
    flat,
    branch_grad,
    inv,
    white,
    branch,
    normed_grad,
    core_send,
    core_recv,
    up_sum,
    down_sum,
    up_recv,
    down_recv,
    core_sems,
    up_sems,
    down_sems,
):
    step = pl.program_id(0)
    pixels, channels = conv_ref.shape
    part = 128
    rest, his, los = extents
    slide, tile = lax.axis_index("slide"), lax.axis_index("tile")
    core, hi, lo = lax.rem(slide, 2), tile // los, lax.rem(tile, los)
    rows = core_send.shape[1] // (his * los)
    core_peer = {"slide": slide + 1 - 2 * core}
    hi_peer = {"tile": (1 - hi) * los + lo}
    lo_next = [lax.rem(lo + offset, los) for offset in range(1, los)]
    lo_peers = [{"tile": hi * los + other} for other in lo_next]

    def remote(source, target, sems, device):
        return pltpu.make_async_remote_copy(
            src_ref=source,
            dst_ref=target,
            send_sem=sems[0],
            recv_sem=sems[1],
            device_id=device,
            device_id_type=pl.DeviceIdType.MESH,
        )

    def core_copy(b):
        sems = (core_sems.at[0, b], core_sems.at[1, b])
        return remote(core_send.at[b], core_recv.at[b], sems, core_peer)

    def up_copy(b):
        sems = (up_sems.at[0, b], up_sems.at[1, b])
        return remote(up_sum.at[b, 1 - hi], up_recv.at[b], sems, hi_peer)

    def down_copy(b, i):
        sems = (down_sems.at[0, b, i], down_sems.at[1, b, i])
        return remote(down_sum.at[b, lo_next[i]], down_recv.at[b, i], sems, lo_peers[i])

    @pl.when(step == 0)
    def _():
        barrier = pltpu.get_barrier_semaphore()
        peers = [core_peer, hi_peer] + lo_peers
        for peer in peers:
            pl.semaphore_signal(
                barrier, inc=1, device_id=peer, device_id_type=pl.DeviceIdType.MESH
            )
        pl.semaphore_wait(barrier, len(peers))

    @pl.when(step == 0)
    def _():
        keep = keep_ref[0:1, 0:1]

        def body(i, total):
            at = pl.ds(pl.multiple_of(i * part, part), part)
            values = conv_ref[at, :]
            centred = values - jnp.mean(values, axis=-1, keepdims=True)
            inv_std = lax.rsqrt(jnp.mean(centred * centred, axis=-1, keepdims=True) + ln_eps)
            whitened = centred * inv_std
            white[at, :] = whitened
            inv[at, :] = jnp.broadcast_to(inv_std, (part, lanes))
            flat[at, :] = (whitened * gain_ref[...] + shift_ref[...]).astype(jnp.bfloat16)
            own = (keep * scale_ref[...] * g_ref[at, :].astype(jnp.float32)).astype(jnp.bfloat16)
            branch_grad[at, :] = own
            return total + jnp.sum(own.astype(jnp.float32), axis=0, keepdims=True)

        zero = jnp.zeros((1, channels), jnp.float32)
        sums_ref[2:3, :] = lax.fori_loop(0, pixels // part, body, zero)
        branch[...] = jnp.zeros_like(branch)
        normed_grad[...] = jnp.zeros_like(normed_grad)

    up = up_ref[...]
    down = down_ref[0] if len(down_ref.shape) == 3 else down_ref[...]
    pre = nt(flat[...], up) + up_bias_ref[0]
    act_grad = nn(branch_grad[...], down)
    cdf = 0.5 * (1.0 + lax.erf(pre * root_half))
    slope = cdf + pre * inv_root_two_pi * jnp.exp(-0.5 * pre * pre)
    act = (pre * cdf).astype(jnp.bfloat16)
    pre_grad_wide = act_grad * slope
    pre_grad = pre_grad_wide.astype(jnp.bfloat16)
    branch[...] += nt(act, down)
    normed_grad[...] += nn(pre_grad, up)
    bias_ref[0] = jnp.sum(pre_grad.astype(jnp.float32), axis=0, keepdims=True)
    up_grad = nn(pre_grad.T, flat[...])
    down_grad = nn(act.T, branch_grad[...])

    @pl.when(step < rest)
    def _():
        core_send[step, :, 0:channels] = up_grad.astype(jnp.bfloat16)
        core_send[step, :, channels : 2 * channels] = down_grad.astype(jnp.bfloat16)
        core_copy(step).start()

    @pl.when(step >= rest)
    def _():
        b = step - rest
        core_copy(b).wait_recv()
        up_total = up_grad + core_recv[b, :, 0:channels].astype(jnp.float32)
        down_total = down_grad + core_recv[b, :, channels : 2 * channels].astype(jnp.float32)
        for h in range(his):
            for l in range(los):
                at = (h * los + l) * rows
                up_sum[b, h, l] = up_total[at : at + rows].astype(jnp.bfloat16)
                down_sum[b, l, h] = down_total[at : at + rows].astype(jnp.bfloat16)
        up_copy(b).start()
        for i in range(los - 1):
            down_copy(b, i).start()

    @pl.when(step == pl.num_programs(0) - 1)
    def _():
        keep = keep_ref[0:1, 0:1]

        def body(i, totals):
            at = pl.ds(pl.multiple_of(i * part, part), part)
            out = branch[at, :] + down_bias_ref[...]
            g = g_ref[at, :].astype(jnp.float32)
            block_out_ref[at, :] = (
                x_ref[at, :].astype(jnp.float32) + keep * scale_ref[...] * out
            ).astype(jnp.bfloat16)
            whitened = white[at, :]
            own = normed_grad[at, :]
            scaled = own * gain_ref[...]
            spread = whitened * jnp.mean(scaled * whitened, axis=-1, keepdims=True)
            centred = scaled - jnp.mean(scaled, axis=-1, keepdims=True) - spread
            conv_grad_ref[at, :] = (inv[at, 0:1] * centred).astype(jnp.bfloat16)
            down_sum = lambda v: jnp.sum(v, axis=0, keepdims=True)
            terms = (own * whitened, own, g * keep * out)
            return tuple(t + down_sum(v) for t, v in zip(totals, terms))

        zero = jnp.zeros((1, channels), jnp.float32)
        totals = lax.fori_loop(0, pixels // part, body, (zero,) * 3)
        sums_ref[0:1, :] = totals[0]
        sums_ref[1:2, :] = totals[1]
        sums_ref[3:4, :] = totals[2]

        def finish(b, carry):
            core_copy(b).wait_send()
            up_copy(b).wait()
            total = up_sum[b, hi].astype(jnp.float32) + up_recv[b].astype(jnp.float32)
            up_grad_ref[b] = total.astype(jnp.bfloat16)
            total = down_sum[b, lo].astype(jnp.float32)
            for i in range(los - 1):
                down_copy(b, i).wait()
                total = total + down_recv[b, i].astype(jnp.float32)
            down_grad_ref[b] = total.astype(jnp.bfloat16)
            return carry

        lax.fori_loop(0, rest, finish, 0)


def mlp(conv, x, g, keep, gain, shift, up, up_bias, down, down_bias, scale, slides, tiles):
    pixels, channels = conv.shape
    hidden = up.shape[0]
    rest, his, los = slides // 2, 2, tiles // 2
    blocks = 2 * rest
    block = hidden // blocks
    rows = block // tiles
    single = pl.Buffered(buffer_count=1)
    whole = lambda shape: pl.BlockSpec(
        shape, lambda j: (0,) * len(shape), pipeline_mode=single
    )
    row = pl.BlockSpec((1, channels), lambda j: (0, 0))

    def at(j):
        core = lax.rem(lax.axis_index("slide"), 2)
        return lax.rem(j, rest) * 2 + jnp.where(j < rest, 1 - core, core)

    if block % lanes == 0:
        down_spec = pl.BlockSpec((channels, block), lambda j: (0, at(j)))
    else:
        down = jnp.transpose(down.reshape(channels, blocks, block), (1, 0, 2))
        down_spec = pl.BlockSpec((1, channels, block), lambda j: (at(j), 0, 0))
    bias_spec = pl.BlockSpec((1, 1, block), lambda j: (at(j), 0, 0))
    shape = jax.ShapeDtypeStruct
    wide, narrow = jnp.float32, jnp.bfloat16
    return pl.pallas_call(
        functools.partial(mlp_body, (rest, his, los)),
        out_shape=(
            shape((pixels, channels), narrow),
            shape((pixels, channels), narrow),
            shape((rest, los, rows, channels), narrow),
            shape((rest, his, rows, channels), narrow),
            shape((4, channels), wide),
            shape((blocks, 1, block), wide),
        ),
        grid=(blocks,),
        in_specs=[
            whole((pixels, channels)),
            whole((pixels, channels)),
            whole((pixels, channels)),
            pl.BlockSpec((1, lanes), lambda j: (0, 0)),
            row,
            row,
            pl.BlockSpec((block, channels), lambda j: (at(j), 0)),
            bias_spec,
            down_spec,
            row,
            row,
        ],
        out_specs=(
            whole((pixels, channels)),
            whole((pixels, channels)),
            whole((rest, los, rows, channels)),
            whole((rest, his, rows, channels)),
            pl.BlockSpec((4, channels), lambda j: (0, 0)),
            bias_spec,
        ),
        scratch_shapes=[
            pltpu.VMEM((pixels, channels), narrow),
            pltpu.VMEM((pixels, channels), narrow),
            pltpu.VMEM((pixels, lanes), wide),
            pltpu.VMEM((pixels, channels), wide),
            pltpu.VMEM((pixels, channels), wide),
            pltpu.VMEM((pixels, channels), wide),
            pltpu.VMEM((rest, block, 2 * channels), narrow),
            pltpu.VMEM((rest, block, 2 * channels), narrow),
            pltpu.VMEM((rest, his, los, rows, channels), narrow),
            pltpu.VMEM((rest, los, his, rows, channels), narrow),
            pltpu.VMEM((rest, los, rows, channels), narrow),
            pltpu.VMEM((rest, los - 1, his, rows, channels), narrow),
            pltpu.SemaphoreType.DMA((2, rest)),
            pltpu.SemaphoreType.DMA((2, rest)),
            pltpu.SemaphoreType.DMA((2, rest, los - 1)),
        ],
        compiler_params=params(collective_id=2, has_side_effects=True),
        cost_estimate=pl.CostEstimate(
            flops=12 * pixels * channels * hidden,
            bytes_accessed=32 << 20,
            transcendentals=2 * pixels * hidden,
        ),
        name="mlp",
    )(conv, x, g, keep, gain, shift, up, up_bias.reshape(blocks, 1, block), down, down_bias, scale)


class Grid:
    def __init__(self, slides, tiles):
        self.sizes = {"rest": slides // 2, "core": 2, "hi": 2, "lo": tiles // 2}
        self.names = ("rest", "core", "hi", "lo")
        slide, tile = lax.axis_index("slide"), lax.axis_index("tile")
        self.place = {
            "rest": slide // 2,
            "core": lax.rem(slide, 2),
            "hi": tile // (tiles // 2),
            "lo": lax.rem(tile, tiles // 2),
        }

    def perm(self, axis, move):
        pairs = []
        extents = [self.sizes[n] for n in self.names]
        at = self.names.index(axis)
        stride = 1
        for size in extents[at + 1 :]:
            stride *= size
        total = 1
        for size in extents:
            total *= size
        for device in range(total):
            own = (device // stride) % extents[at]
            pairs.append((device, device + (move(own) - own) * stride))
        return pairs

    def send(self, value, axis, move):
        return lax.ppermute(value, ("slide", "tile"), self.perm(axis, move))

    def scatter(self, value, dim, axis, last=False):
        size, own = self.sizes[axis], self.place[axis]
        pick = lambda i: lax.dynamic_index_in_dim(value, i, dim, keepdims=False)
        total = pick(own).astype(jnp.float32)
        for offset in range(1, size):
            block = pick(lax.rem(own + offset, size))
            came = self.send(block, axis, lambda i, o=offset: (i + o) % size)
            total = total + came.astype(jnp.float32)
        return total if last else total.astype(jnp.bfloat16)

    def everywhere(self, value):
        for axis in self.names[::-1]:
            step = 1
            while step < self.sizes[axis]:
                value = value + self.send(value, axis, lambda i, s=step: i ^ s)
                step *= 2
        return value


def on_device(
    features,
    cotangent,
    neighbours,
    skip_flags,
    dw_weight,
    ln_gain,
    ln_bias,
    up_weight,
    up_bias,
    down_weight,
    down_bias,
    layer_scale,
):
    slides, tiles = lax.axis_size("slide"), lax.axis_size("tile")
    side, channels = features.shape[3], features.shape[4]
    hidden = up_weight.shape[1]
    table = neighbours[0]
    grid = Grid(slides, tiles)
    tile, grad = features[0, 0], cotangent[0, 0]
    taps = dw_weight[0].reshape(49, channels)
    keep = jnp.broadcast_to((1 - skip_flags[0, 0]).astype(jnp.float32), (1, lanes))

    rims = exchange_rims(tile, table, tiles, 0)
    conv = depthwise(tile, rims, taps)
    block_out, conv_grad, up_grad, down_grad, sums, bias = mlp(
        conv.reshape(-1, channels),
        tile.reshape(-1, channels),
        grad.reshape(-1, channels),
        keep,
        ln_gain,
        ln_bias,
        up_weight[0],
        up_bias,
        down_weight[0],
        down_bias,
        layer_scale,
        slides,
        tiles,
    )
    conv_tile = conv_grad.reshape(side, side, channels)
    grad_rims = exchange_rims(conv_tile, table, tiles, 1)

    up_part = grid.scatter(up_grad, 1, "lo")
    down_part = grid.scatter(down_grad, 1, "hi")
    up_part = grid.scatter(up_part, 0, "rest", last=True)
    down_part = grid.scatter(down_part, 0, "rest", last=True)
    weight_grads = jnp.concatenate([up_part, down_part], -1)[None]

    kernel_sum = kernel_grad(tile, rims, conv_tile)
    small = jnp.concatenate([kernel_sum, sums, bias.reshape(-1, channels)], 0)
    small = grid.everywhere(small)
    input_grad = depthwise(conv_tile, grad_rims, taps[::-1], grad)
    return (
        block_out.reshape(1, 1, side, side, channels),
        input_grad[None, None],
        weight_grads,
        small[:49].reshape(1, 7, 7, channels),
        small[49:53][None],
        small[53:].reshape(1, hidden),
    )


def solution(mesh):
    tiles = P("slide", "tile", None, None, None)
    return jax.shard_map(
        on_device,
        mesh=mesh,
        in_specs=(tiles, tiles, P("slide", None, None), P(None, "slide")) + (P(),) * 8,
        out_specs=(tiles, tiles, P(None, ("slide", "tile"), None), P(), P(), P()),
        check_vma=False,
    )
```

```python
import functools

import jax
import jax.numpy as jnp
from jax import lax
from jax.experimental import pallas as pl
from jax.experimental.pallas import tpu as pltpu
from jax.sharding import PartitionSpec as P

ln_eps = 1e-06
root_half = 0.7071067811865476
inv_root_two_pi = 0.3989422804014327
kind_of = (0, 1, 2, 3, 0, 0, 1, 1)
lanes = 128
row_step = 4
vmem_bytes = 60 * 1024 * 1024


def params(**more):
    return pltpu.CompilerParams(vmem_limit_bytes=vmem_bytes, **more)


def rim_body(
    count, table, tile, top, bottom, west, east, strips, sends, slots, send_sem, recv_sem
):
    side = tile.shape[0]
    me = lax.axis_index("tile")
    peers = [lax.rem(me + offset, count) for offset in range(1, count)]
    barrier = pltpu.get_barrier_semaphore()
    for peer in peers:
        pl.semaphore_signal(
            barrier, inc=1, device_id={"tile": peer}, device_id_type=pl.DeviceIdType.MESH
        )
    for k in range(3):
        at = pl.ds(k * side, side)
        strips[0, at] = tile[side - 3 + k].astype(jnp.float32)
        strips[1, at] = tile[k].astype(jnp.float32)
    for h in range(side):
        row = tile[h].astype(jnp.float32)
        strips[2, 3 * h : 3 * h + 3] = row[side - 3 :]
        strips[3, 3 * h : 3 * h + 3] = row[:3]
    slots[0] = jnp.zeros(slots.shape[1:], slots.dtype)
    pl.semaphore_wait(barrier, count - 1)
    copies = []
    for i, peer in enumerate(peers):
        kind = jnp.int32(0)
        for d in range(8):
            kind = jnp.where(table[peer, d] == me, kind_of[d], kind)
        sends[i] = strips[kind].astype(jnp.bfloat16)
        copy = pltpu.make_async_remote_copy(
            src_ref=sends.at[i],
            dst_ref=slots.at[i + 1],
            send_sem=send_sem.at[i],
            recv_sem=recv_sem.at[i],
            device_id={"tile": peer},
            device_id_type=pl.DeviceIdType.MESH,
        )
        copy.start()
        copies.append(copy)
    top[...] = jnp.zeros_like(top)
    bottom[...] = jnp.zeros_like(bottom)
    west[...] = jnp.zeros_like(west)
    east[...] = jnp.zeros_like(east)
    for copy in copies:
        copy.wait()

    def load(slot, d):
        other = table[me, d]
        place = jnp.where(other == count, 0, lax.rem(me - other + count, count))
        strips[slot] = slots[place].astype(jnp.float32)

    for edge, (left, centre, right) in ((top, (4, 0, 5)), (bottom, (6, 1, 7))):
        load(0, left)
        load(1, centre)
        load(2, right)
        for k in range(3):
            edge[k, 5:8] = strips[0, k * side + side - 3 : k * side + side]
            edge[k, 8 : 8 + side] = strips[1, k * side : k * side + side]
            edge[k, 8 + side : 11 + side] = strips[2, k * side : k * side + 3]
    load(0, 2)
    load(1, 3)
    for h in range(side):
        west[h, 5:8] = strips[0, 3 * h : 3 * h + 3]
        east[h, 0:3] = strips[1, 3 * h : 3 * h + 3]


def exchange_rims(tile, table, count, call):
    side, _, channels = tile.shape
    vmem = pl.BlockSpec(memory_space=pltpu.VMEM)
    edge = jax.ShapeDtypeStruct((3, side + 16, channels), jnp.float32)
    flank = jax.ShapeDtypeStruct((side, 8, channels), jnp.float32)
    return pl.pallas_call(
        functools.partial(rim_body, count),
        out_shape=(edge, edge, flank, flank),
        in_specs=[pl.BlockSpec(memory_space=pltpu.SMEM), vmem],
        out_specs=(vmem,) * 4,
        scratch_shapes=[
            pltpu.VMEM((4, 3 * side, channels), jnp.float32),
            pltpu.VMEM((count - 1, 3 * side, channels), jnp.bfloat16),
            pltpu.VMEM((count, 3 * side, channels), jnp.bfloat16),
            pltpu.SemaphoreType.DMA((count - 1,)),
            pltpu.SemaphoreType.DMA((count - 1,)),
        ],
        compiler_params=params(collective_id=call, has_side_effects=True),
        cost_estimate=pl.CostEstimate(
            flops=10**10, bytes_accessed=8 << 20, transcendentals=0
        ),
        name="rims" + str(call),
    )(table, tile)


def fill(ext, tile_ref, top_ref, bottom_ref, west_ref, east_ref):
    side = tile_ref.shape[0]
    ext[0:3] = top_ref[...]
    ext[side + 3 : side + 6] = bottom_ref[...]
    ext[3 : side + 3, 0:8] = west_ref[...]
    ext[3 : side + 3, 8 : side + 8] = tile_ref[...].astype(jnp.float32)
    ext[3 : side + 3, side + 8 : side + 16] = east_ref[...]


def conv_body(tile_ref, top, bottom, west, east, weight_ref, out_ref, ext, shifted, total):
    conv_sum(tile_ref, top, bottom, west, east, weight_ref, ext, shifted, total)
    out_ref[...] = total[...]


def conv_sum(tile_ref, top, bottom, west, east, weight_ref, ext, shifted, total):
    side = tile_ref.shape[0]
    fill(ext, tile_ref, top, bottom, west, east)
    for b in range(7):
        if b == 3:
            source, base = ext, 8
        else:
            shifted[...] = ext[:, 5 + b : 5 + b + side]
            source, base = shifted, 0
        taps = [
            jnp.broadcast_to(weight_ref[a * 7 + b : a * 7 + b + 1, :], (8, lanes)) for a in range(7)
        ]

        def rows(step, carry, b=b, source=source, base=base, taps=taps):
            first = step * row_step
            for group in range(side // 8):
                at = pl.ds(base + group * 8, 8)
                here = pl.ds(group * 8, 8)
                sums = [None] * row_step
                for r in range(row_step + 6):
                    value = source[first + r, at]
                    for i in range(row_step):
                        a = r - i
                        if 0 <= a < 7:
                            term = value * taps[a]
                            sums[i] = term if sums[i] is None else sums[i] + term
                for i in range(row_step):
                    if b > 0:
                        sums[i] = sums[i] + total[first + i, here]
                    total[first + i, here] = sums[i]
            return carry

        lax.fori_loop(0, side // row_step, rows, 0)


def back_body(
    extents,
    tile_ref,
    top,
    bottom,
    west,
    east,
    weight_ref,
    add_ref,
    up,
    down,
    small,
    out_ref,
    up_out,
    down_out,
    small_out,
    ext,
    shifted,
    total,
    up_recv,
    down_recv,
    small_recv,
    slide_slots,
    tile_slots,
    up_sems,
    down_sems,
    small_sems,
    slide_sems,
    tile_sems,
):
    slides, tiles = extents
    rest = slides // 2
    step = pl.program_id(0)
    slide, tile = lax.axis_index("slide"), lax.axis_index("tile")
    far, core = slide // 2, lax.rem(slide, 2)
    next_tile = [lax.rem(tile + o, tiles) for o in range(1, tiles)]
    next_slide = [lax.rem(slide + o, slides) for o in range(1, slides)]
    next_far = [lax.rem(far + o, rest) for o in range(1, rest)]

    def remote(source, target, sems, i, device):
        return pltpu.make_async_remote_copy(
            src_ref=source,
            dst_ref=target,
            send_sem=sems.at[0, i],
            recv_sem=sems.at[1, i],
            device_id=device,
            device_id_type=pl.DeviceIdType.MESH,
        )

    def far_copies(part, recv, sems):
        return [
            remote(part.at[at], recv.at[i], sems, i, {"slide": at * 2 + core})
            for i, at in enumerate(next_far)
        ]

    def small_copies():
        return [
            remote(small.at[at], small_recv.at[i], small_sems, i, {"tile": at})
            for i, at in enumerate(next_tile)
        ]

    def slide_copies():
        return [
            remote(slide_slots.at[0], slide_slots.at[i + 1], slide_sems, i, {"slide": at})
            for i, at in enumerate(next_slide)
        ]

    def tile_copies():
        return [
            remote(tile_slots.at[0], tile_slots.at[i + 1], tile_sems, i, {"tile": at})
            for i, at in enumerate(next_tile)
        ]

    @pl.when(step == 0)
    def _():
        barrier = pltpu.get_barrier_semaphore()
        peers = [{"tile": at} for at in next_tile] + [{"slide": at} for at in next_slide]
        for peer in peers:
            pl.semaphore_signal(
                barrier, inc=1, device_id=peer, device_id_type=pl.DeviceIdType.MESH
            )
        pl.semaphore_wait(barrier, len(peers))
        for copy in small_copies() + far_copies(up, up_recv, up_sems):
            copy.start()

    @pl.when(step == 1)
    def _():
        own = small[tile]
        for i, copy in enumerate(small_copies()):
            copy.wait()
            own = own + small_recv[i]
        slide_slots[0] = own
        for copy in slide_copies() + far_copies(down, down_recv, down_sems):
            copy.start()

    @pl.when(step == 4)
    def _():
        for copy in slide_copies():
            copy.wait()
        own = slide_slots[lax.rem(slide, slides)]
        for i in range(1, slides):
            own = own + slide_slots[lax.rem(slide - i + slides, slides)]
        tile_slots[0] = own
        for copy in tile_copies():
            copy.start()

    conv_sum(tile_ref, top, bottom, west, east, weight_ref, ext, shifted, total)
    out_ref[...] = (add_ref[...].astype(jnp.float32) + total[...]).astype(jnp.bfloat16)

    @pl.when(step == pl.num_programs(0) - 1)
    def _():
        for copy in tile_copies():
            copy.wait()
        for i in range(tiles):
            small_out[i] = tile_slots[lax.rem(tile - i + tiles, tiles)]
        for part, recv, sems, out in (
            (up, up_recv, up_sems, up_out),
            (down, down_recv, down_sems, down_out),
        ):
            out[...] = part[far].astype(jnp.float32)
            for i, copy in enumerate(far_copies(part, recv, sems)):
                copy.wait()
                out[...] += recv[i].astype(jnp.float32)


def depthwise_and_sums(tile, rims, weight, add, up, down, small, slides, tiles):
    side, _, channels = tile.shape
    rest, rows = up.shape[0], up.shape[1]
    chunk = small.shape[1]
    operands = [tile, *rims, weight, add]
    fixed = lambda shape: pl.BlockSpec(
        shape, lambda c: (0,) * len(shape), pipeline_mode=pl.Buffered(buffer_count=1)
    )
    shape = jax.ShapeDtypeStruct
    wide, narrow = jnp.float32, jnp.bfloat16
    return pl.pallas_call(
        functools.partial(back_body, (slides, tiles)),
        out_shape=(
            shape(tile.shape, narrow),
            shape((rows, channels), wide),
            shape((rows, channels), wide),
            shape(small.shape, wide),
        ),
        grid=(channels // lanes,),
        in_specs=[tile_spec(o.shape) for o in operands]
        + [fixed(up.shape), fixed(down.shape), fixed(small.shape)],
        out_specs=(
            tile_spec(tile.shape),
            fixed((rows, channels)),
            fixed((rows, channels)),
            fixed(small.shape),
        ),
        scratch_shapes=[
            pltpu.VMEM((side + 6, side + 16, lanes), wide),
            pltpu.VMEM((side + 6, side, lanes), wide),
            pltpu.VMEM((side, side, lanes), wide),
            pltpu.VMEM((rest - 1, rows, channels), narrow),
            pltpu.VMEM((rest - 1, rows, channels), narrow),
            pltpu.VMEM((tiles - 1, chunk, channels), wide),
            pltpu.VMEM((slides, chunk, channels), wide),
            pltpu.VMEM((tiles, chunk, channels), wide),
            pltpu.SemaphoreType.DMA((2, rest - 1)),
            pltpu.SemaphoreType.DMA((2, rest - 1)),
            pltpu.SemaphoreType.DMA((2, tiles - 1)),
            pltpu.SemaphoreType.DMA((2, slides - 1)),
            pltpu.SemaphoreType.DMA((2, tiles - 1)),
        ],
        compiler_params=params(collective_id=3, has_side_effects=True),
        cost_estimate=pl.CostEstimate(
            flops=2 * 10**10, bytes_accessed=8 << 20, transcendentals=0
        ),
        name="depthwise_and_sums",
    )(*operands, up, down, small)


def tile_spec(shape):
    return pl.BlockSpec(shape[:-1] + (lanes,), lambda c: (0,) * (len(shape) - 1) + (c,))


def depthwise(tile, rims, weight):
    side, _, channels = tile.shape
    operands = [tile, *rims, weight]
    flops = 2 * 49 * side * side * channels
    return pl.pallas_call(
        conv_body,
        out_shape=jax.ShapeDtypeStruct(tile.shape, jnp.float32),
        grid=(channels // lanes,),
        in_specs=[tile_spec(o.shape) for o in operands],
        out_specs=tile_spec(tile.shape),
        scratch_shapes=[
            pltpu.VMEM((side + 6, side + 16, lanes), jnp.float32),
            pltpu.VMEM((side + 6, side, lanes), jnp.float32),
            pltpu.VMEM((side, side, lanes), jnp.float32),
        ],
        compiler_params=params(),
        cost_estimate=pl.CostEstimate(flops=260 * flops, bytes_accessed=8 << 20, transcendentals=0),
        name="depthwise",
    )(*operands)


def kernel_grad_body(tile_ref, top, bottom, west, east, grad_ref, out_ref, ext, shifted, grad):
    side = tile_ref.shape[0]
    fill(ext, tile_ref, top, bottom, west, east)
    grad[...] = grad_ref[...].astype(jnp.float32)
    for b in range(7):
        if b == 3:
            source, base = ext, 8
        else:
            shifted[...] = ext[:, 5 + b : 5 + b + side]
            source, base = shifted, 0

        def rows(step, sums, source=source, base=base):
            first = step * row_step
            sums = list(sums)
            for group in range(side // 8):
                at = pl.ds(base + group * 8, 8)
                here = pl.ds(group * 8, 8)
                near = [grad[first + i, here] for i in range(row_step)]
                for r in range(row_step + 6):
                    value = source[first + r, at]
                    for i in range(row_step):
                        a = r - i
                        if 0 <= a < 7:
                            slot = a * 2 + i % 2
                            sums[slot] = sums[slot] + value * near[i]
            return tuple(sums)

        zero = jnp.zeros((8, lanes), jnp.float32)
        sums = lax.fori_loop(0, side // row_step, rows, (zero,) * 14)
        for a in range(7):
            out_ref[a * 7 + b : a * 7 + b + 1, :] = jnp.sum(
                sums[2 * a] + sums[2 * a + 1], axis=0, keepdims=True
            )


def kernel_grad(tile, rims, conv_grad):
    side, _, channels = tile.shape
    operands = [tile, *rims, conv_grad]
    flops = 2 * 49 * side * side * channels
    return pl.pallas_call(
        kernel_grad_body,
        out_shape=jax.ShapeDtypeStruct((49, channels), jnp.float32),
        grid=(channels // lanes,),
        in_specs=[tile_spec(o.shape) for o in operands],
        out_specs=tile_spec((49, channels)),
        scratch_shapes=[
            pltpu.VMEM((side + 6, side + 16, lanes), jnp.float32),
            pltpu.VMEM((side + 6, side, lanes), jnp.float32),
            pltpu.VMEM((side, side, lanes), jnp.float32),
        ],
        compiler_params=params(),
        cost_estimate=pl.CostEstimate(flops=260 * flops, bytes_accessed=8 << 20, transcendentals=0),
        name="kernel_grad",
    )(*operands)


def nt(left, right):
    return lax.dot_general(
        left, right, (((1,), (1,)), ((), ())), preferred_element_type=jnp.float32
    )


def nn(left, right):
    return jnp.dot(left, right, preferred_element_type=jnp.float32)


def mlp_body(
    extents,
    conv_ref,
    x_ref,
    g_ref,
    keep_ref,
    gain_ref,
    shift_ref,
    up_ref,
    up_bias_ref,
    down_ref,
    down_bias_ref,
    scale_ref,
    block_out_ref,
    conv_grad_ref,
    up_grad_ref,
    down_grad_ref,
    sums_ref,
    bias_ref,
    flat,
    branch_grad,
    inv,
    white,
    branch,
    normed_grad,
    core_send,
    core_recv,
    up_sum,
    down_sum,
    up_recv,
    down_recv,
    core_sems,
    up_sems,
    down_sems,
):
    step = pl.program_id(0)
    pixels, channels = conv_ref.shape
    part = 128
    rest, his, los = extents
    slide, tile = lax.axis_index("slide"), lax.axis_index("tile")
    core, hi, lo = lax.rem(slide, 2), tile // los, lax.rem(tile, los)
    rows = core_send.shape[1] // (his * los)
    core_peer = {"slide": slide + 1 - 2 * core}
    hi_peer = {"tile": (1 - hi) * los + lo}
    lo_next = [lax.rem(lo + offset, los) for offset in range(1, los)]
    lo_peers = [{"tile": hi * los + other} for other in lo_next]

    def remote(source, target, sems, device):
        return pltpu.make_async_remote_copy(
            src_ref=source,
            dst_ref=target,
            send_sem=sems[0],
            recv_sem=sems[1],
            device_id=device,
            device_id_type=pl.DeviceIdType.MESH,
        )

    def core_copy(b):
        sems = (core_sems.at[0, b], core_sems.at[1, b])
        return remote(core_send.at[b], core_recv.at[b], sems, core_peer)

    def up_copy(b):
        sems = (up_sems.at[0, b], up_sems.at[1, b])
        return remote(up_sum.at[b, 1 - hi], up_recv.at[b], sems, hi_peer)

    def down_copy(b, i):
        sems = (down_sems.at[0, b, i], down_sems.at[1, b, i])
        return remote(down_sum.at[b, lo_next[i]], down_recv.at[b, i], sems, lo_peers[i])

    @pl.when(step == 0)
    def _():
        barrier = pltpu.get_barrier_semaphore()
        peers = [core_peer, hi_peer] + lo_peers
        for peer in peers:
            pl.semaphore_signal(
                barrier, inc=1, device_id=peer, device_id_type=pl.DeviceIdType.MESH
            )
        pl.semaphore_wait(barrier, len(peers))

    @pl.when(step == 0)
    def _():
        keep = keep_ref[0:1, 0:1]

        def body(i, total):
            at = pl.ds(pl.multiple_of(i * part, part), part)
            values = conv_ref[at, :]
            centred = values - jnp.mean(values, axis=-1, keepdims=True)
            inv_std = lax.rsqrt(jnp.mean(centred * centred, axis=-1, keepdims=True) + ln_eps)
            whitened = centred * inv_std
            white[at, :] = whitened
            inv[at, :] = jnp.broadcast_to(inv_std, (part, lanes))
            flat[at, :] = (whitened * gain_ref[...] + shift_ref[...]).astype(jnp.bfloat16)
            own = (keep * scale_ref[...] * g_ref[at, :].astype(jnp.float32)).astype(jnp.bfloat16)
            branch_grad[at, :] = own
            return total + jnp.sum(own.astype(jnp.float32), axis=0, keepdims=True)

        zero = jnp.zeros((1, channels), jnp.float32)
        sums_ref[2:3, :] = lax.fori_loop(0, pixels // part, body, zero)
        branch[...] = jnp.zeros_like(branch)
        normed_grad[...] = jnp.zeros_like(normed_grad)

    up = up_ref[...]
    down = down_ref[0] if len(down_ref.shape) == 3 else down_ref[...]
    pre = nt(flat[...], up) + up_bias_ref[0]
    act_grad = nn(branch_grad[...], down)
    cdf = 0.5 * (1.0 + lax.erf(pre * root_half))
    slope = cdf + pre * inv_root_two_pi * jnp.exp(-0.5 * pre * pre)
    act = (pre * cdf).astype(jnp.bfloat16)
    pre_grad_wide = act_grad * slope
    pre_grad = pre_grad_wide.astype(jnp.bfloat16)
    branch[...] += nt(act, down)
    normed_grad[...] += nn(pre_grad, up)
    bias_ref[0] = jnp.sum(pre_grad.astype(jnp.float32), axis=0, keepdims=True)
    up_grad = nn(pre_grad.T, flat[...])
    down_grad = nn(act.T, branch_grad[...])

    @pl.when(step < rest)
    def _():
        core_send[step, :, 0:channels] = up_grad.astype(jnp.bfloat16)
        core_send[step, :, channels : 2 * channels] = down_grad.astype(jnp.bfloat16)
        core_copy(step).start()

    @pl.when(step >= rest)
    def _():
        b = step - rest
        core_copy(b).wait_recv()
        up_total = up_grad + core_recv[b, :, 0:channels].astype(jnp.float32)
        down_total = down_grad + core_recv[b, :, channels : 2 * channels].astype(jnp.float32)
        for h in range(his):
            for l in range(los):
                at = (h * los + l) * rows
                up_sum[b, h, l] = up_total[at : at + rows].astype(jnp.bfloat16)
                down_sum[b, l, h] = down_total[at : at + rows].astype(jnp.bfloat16)
        up_copy(b).start()
        for i in range(los - 1):
            down_copy(b, i).start()

    @pl.when(step == pl.num_programs(0) - 1)
    def _():
        keep = keep_ref[0:1, 0:1]

        def body(i, totals):
            at = pl.ds(pl.multiple_of(i * part, part), part)
            out = branch[at, :] + down_bias_ref[...]
            g = g_ref[at, :].astype(jnp.float32)
            block_out_ref[at, :] = (
                x_ref[at, :].astype(jnp.float32) + keep * scale_ref[...] * out
            ).astype(jnp.bfloat16)
            whitened = white[at, :]
            own = normed_grad[at, :]
            scaled = own * gain_ref[...]
            spread = whitened * jnp.mean(scaled * whitened, axis=-1, keepdims=True)
            centred = scaled - jnp.mean(scaled, axis=-1, keepdims=True) - spread
            conv_grad_ref[at, :] = (inv[at, 0:1] * centred).astype(jnp.bfloat16)
            down_sum = lambda v: jnp.sum(v, axis=0, keepdims=True)
            terms = (own * whitened, own, g * keep * out)
            return tuple(t + down_sum(v) for t, v in zip(totals, terms))

        zero = jnp.zeros((1, channels), jnp.float32)
        totals = lax.fori_loop(0, pixels // part, body, (zero,) * 3)
        sums_ref[0:1, :] = totals[0]
        sums_ref[1:2, :] = totals[1]
        sums_ref[3:4, :] = totals[2]

        def finish(b, carry):
            core_copy(b).wait_send()
            up_copy(b).wait()
            total = up_sum[b, hi].astype(jnp.float32) + up_recv[b].astype(jnp.float32)
            up_grad_ref[b] = total.astype(jnp.bfloat16)
            total = down_sum[b, lo].astype(jnp.float32)
            for i in range(los - 1):
                down_copy(b, i).wait()
                total = total + down_recv[b, i].astype(jnp.float32)
            down_grad_ref[b] = total.astype(jnp.bfloat16)
            return carry

        lax.fori_loop(0, rest, finish, 0)


def mlp(conv, x, g, keep, gain, shift, up, up_bias, down, down_bias, scale, slides, tiles):
    pixels, channels = conv.shape
    hidden = up.shape[0]
    rest, his, los = slides // 2, 2, tiles // 2
    blocks = 2 * rest
    block = hidden // blocks
    rows = block // tiles
    single = pl.Buffered(buffer_count=1)
    whole = lambda shape: pl.BlockSpec(
        shape, lambda j: (0,) * len(shape), pipeline_mode=single
    )
    row = pl.BlockSpec((1, channels), lambda j: (0, 0))

    def at(j):
        core = lax.rem(lax.axis_index("slide"), 2)
        return lax.rem(j, rest) * 2 + jnp.where(j < rest, 1 - core, core)

    if block % lanes == 0:
        down_spec = pl.BlockSpec((channels, block), lambda j: (0, at(j)))
    else:
        down = jnp.transpose(down.reshape(channels, blocks, block), (1, 0, 2))
        down_spec = pl.BlockSpec((1, channels, block), lambda j: (at(j), 0, 0))
    bias_spec = pl.BlockSpec((1, 1, block), lambda j: (at(j), 0, 0))
    shape = jax.ShapeDtypeStruct
    wide, narrow = jnp.float32, jnp.bfloat16
    return pl.pallas_call(
        functools.partial(mlp_body, (rest, his, los)),
        out_shape=(
            shape((pixels, channels), narrow),
            shape((pixels, channels), narrow),
            shape((rest, los, rows, channels), narrow),
            shape((rest, his, rows, channels), narrow),
            shape((4, channels), wide),
            shape((blocks, 1, block), wide),
        ),
        grid=(blocks,),
        in_specs=[
            whole((pixels, channels)),
            whole((pixels, channels)),
            whole((pixels, channels)),
            pl.BlockSpec((1, lanes), lambda j: (0, 0)),
            row,
            row,
            pl.BlockSpec((block, channels), lambda j: (at(j), 0)),
            bias_spec,
            down_spec,
            row,
            row,
        ],
        out_specs=(
            whole((pixels, channels)),
            whole((pixels, channels)),
            whole((rest, los, rows, channels)),
            whole((rest, his, rows, channels)),
            pl.BlockSpec((4, channels), lambda j: (0, 0)),
            bias_spec,
        ),
        scratch_shapes=[
            pltpu.VMEM((pixels, channels), narrow),
            pltpu.VMEM((pixels, channels), narrow),
            pltpu.VMEM((pixels, lanes), wide),
            pltpu.VMEM((pixels, channels), wide),
            pltpu.VMEM((pixels, channels), wide),
            pltpu.VMEM((pixels, channels), wide),
            pltpu.VMEM((rest, block, 2 * channels), narrow),
            pltpu.VMEM((rest, block, 2 * channels), narrow),
            pltpu.VMEM((rest, his, los, rows, channels), narrow),
            pltpu.VMEM((rest, los, his, rows, channels), narrow),
            pltpu.VMEM((rest, los, rows, channels), narrow),
            pltpu.VMEM((rest, los - 1, his, rows, channels), narrow),
            pltpu.SemaphoreType.DMA((2, rest)),
            pltpu.SemaphoreType.DMA((2, rest)),
            pltpu.SemaphoreType.DMA((2, rest, los - 1)),
        ],
        compiler_params=params(collective_id=2, has_side_effects=True),
        cost_estimate=pl.CostEstimate(
            flops=12 * pixels * channels * hidden,
            bytes_accessed=32 << 20,
            transcendentals=2 * pixels * hidden,
        ),
        name="mlp",
    )(conv, x, g, keep, gain, shift, up, up_bias.reshape(blocks, 1, block), down, down_bias, scale)


class Grid:
    def __init__(self, slides, tiles):
        self.sizes = {"rest": slides // 2, "core": 2, "hi": 2, "lo": tiles // 2}
        self.names = ("rest", "core", "hi", "lo")
        slide, tile = lax.axis_index("slide"), lax.axis_index("tile")
        self.place = {
            "rest": slide // 2,
            "core": lax.rem(slide, 2),
            "hi": tile // (tiles // 2),
            "lo": lax.rem(tile, tiles // 2),
        }

    def perm(self, axis, move):
        pairs = []
        extents = [self.sizes[n] for n in self.names]
        at = self.names.index(axis)
        stride = 1
        for size in extents[at + 1 :]:
            stride *= size
        total = 1
        for size in extents:
            total *= size
        for device in range(total):
            own = (device // stride) % extents[at]
            pairs.append((device, device + (move(own) - own) * stride))
        return pairs

    def send(self, value, axis, move):
        return lax.ppermute(value, ("slide", "tile"), self.perm(axis, move))

    def scatter(self, value, dim, axis, last=False):
        size, own = self.sizes[axis], self.place[axis]
        pick = lambda i: lax.dynamic_index_in_dim(value, i, dim, keepdims=False)
        total = pick(own).astype(jnp.float32)
        for offset in range(1, size):
            block = pick(lax.rem(own + offset, size))
            came = self.send(block, axis, lambda i, o=offset: (i + o) % size)
            total = total + came.astype(jnp.float32)
        return total if last else total.astype(jnp.bfloat16)


def on_device(
    features,
    cotangent,
    neighbours,
    skip_flags,
    dw_weight,
    ln_gain,
    ln_bias,
    up_weight,
    up_bias,
    down_weight,
    down_bias,
    layer_scale,
):
    slides, tiles = lax.axis_size("slide"), lax.axis_size("tile")
    side, channels = features.shape[3], features.shape[4]
    hidden = up_weight.shape[1]
    table = neighbours[0]
    grid = Grid(slides, tiles)
    tile, grad = features[0, 0], cotangent[0, 0]
    taps = dw_weight[0].reshape(49, channels)
    keep = jnp.broadcast_to((1 - skip_flags[0, 0]).astype(jnp.float32), (1, lanes))

    rims = exchange_rims(tile, table, tiles, 0)
    conv = depthwise(tile, rims, taps)
    block_out, conv_grad, up_grad, down_grad, sums, bias = mlp(
        conv.reshape(-1, channels),
        tile.reshape(-1, channels),
        grad.reshape(-1, channels),
        keep,
        ln_gain,
        ln_bias,
        up_weight[0],
        up_bias,
        down_weight[0],
        down_bias,
        layer_scale,
        slides,
        tiles,
    )
    conv_tile = conv_grad.reshape(side, side, channels)
    kernel_sum = kernel_grad(tile, rims, conv_tile)
    up_part = grid.scatter(up_grad, 1, "lo")
    down_part = grid.scatter(down_grad, 1, "hi")
    conv_tile, kernel_sum, up_part, down_part = lax.optimization_barrier(
        (conv_tile, kernel_sum, up_part, down_part)
    )
    small = jnp.concatenate([kernel_sum, sums, bias.reshape(-1, channels)], 0)
    count = small.shape[0]
    small = jnp.pad(small, ((0, -count % (8 * tiles)), (0, 0))).reshape(tiles, -1, channels)
    grad_rims = exchange_rims(conv_tile, table, tiles, 1)
    input_grad, up_part, down_part, small = depthwise_and_sums(
        conv_tile, grad_rims, taps[::-1], grad, up_part, down_part, small, slides, tiles
    )
    small = small.reshape(-1, channels)
    weight_grads = jnp.concatenate([up_part, down_part], -1)[None]
    return (
        block_out.reshape(1, 1, side, side, channels),
        input_grad[None, None],
        weight_grads,
        small[:49].reshape(1, 7, 7, channels),
        small[49:53][None],
        small[53:count].reshape(1, hidden),
    )


def solution(mesh):
    tiles = P("slide", "tile", None, None, None)
    return jax.shard_map(
        on_device,
        mesh=mesh,
        in_specs=(tiles, tiles, P("slide", None, None), P(None, "slide")) + (P(),) * 8,
        out_specs=(tiles, tiles, P(None, ("slide", "tile"), None), P(), P(), P()),
        check_vma=False,
    )
```

```python
import functools

import jax
import jax.numpy as jnp
from jax import lax
from jax.experimental import pallas as pl
from jax.experimental.pallas import tpu as pltpu
from jax.sharding import PartitionSpec as P

ln_eps = 1e-06
root_half = 0.7071067811865476
inv_root_two_pi = 0.3989422804014327
kind_of = (0, 1, 2, 3, 0, 0, 1, 1)
lanes = 128
row_step = 4
vmem_bytes = 60 * 1024 * 1024


def params(**more):
    return pltpu.CompilerParams(vmem_limit_bytes=vmem_bytes, **more)


def rim_body(count, rest, table, tile, *refs):
    if rest:
        part, top, bottom, west, east, part_out, *refs = refs
        strips, sends, slots, send_sem, recv_sem, part_recv, part_sems = refs
    else:
        top, bottom, west, east, strips, sends, slots, send_sem, recv_sem = refs
    slide = lax.axis_index("slide")
    far, core = slide // 2, lax.rem(slide, 2)
    next_far = [lax.rem(far + o, rest) for o in range(1, rest)]
    side = tile.shape[0]
    me = lax.axis_index("tile")
    peers = [lax.rem(me + offset, count) for offset in range(1, count)]
    barrier = pltpu.get_barrier_semaphore()
    for peer in peers:
        pl.semaphore_signal(
            barrier, inc=1, device_id={"tile": peer}, device_id_type=pl.DeviceIdType.MESH
        )
    for at in next_far:
        device = {"slide": at * 2 + core}
        pl.semaphore_signal(
            barrier, inc=1, device_id=device, device_id_type=pl.DeviceIdType.MESH
        )
    for k in range(3):
        at = pl.ds(k * side, side)
        strips[0, at] = tile[side - 3 + k].astype(jnp.float32)
        strips[1, at] = tile[k].astype(jnp.float32)
    for h in range(side):
        row = tile[h].astype(jnp.float32)
        strips[2, 3 * h : 3 * h + 3] = row[side - 3 :]
        strips[3, 3 * h : 3 * h + 3] = row[:3]
    slots[0] = jnp.zeros(slots.shape[1:], slots.dtype)
    pl.semaphore_wait(barrier, count - 1 + len(next_far))
    far_copies = []
    for i, at in enumerate(next_far):
        copy = pltpu.make_async_remote_copy(
            src_ref=part.at[at],
            dst_ref=part_recv.at[i],
            send_sem=part_sems.at[0, i],
            recv_sem=part_sems.at[1, i],
            device_id={"slide": at * 2 + core},
            device_id_type=pl.DeviceIdType.MESH,
        )
        copy.start()
        far_copies.append(copy)
    copies = []
    for i, peer in enumerate(peers):
        kind = jnp.int32(0)
        for d in range(8):
            kind = jnp.where(table[peer, d] == me, kind_of[d], kind)
        sends[i] = strips[kind].astype(jnp.bfloat16)
        copy = pltpu.make_async_remote_copy(
            src_ref=sends.at[i],
            dst_ref=slots.at[i + 1],
            send_sem=send_sem.at[i],
            recv_sem=recv_sem.at[i],
            device_id={"tile": peer},
            device_id_type=pl.DeviceIdType.MESH,
        )
        copy.start()
        copies.append(copy)
    top[...] = jnp.zeros_like(top)
    bottom[...] = jnp.zeros_like(bottom)
    west[...] = jnp.zeros_like(west)
    east[...] = jnp.zeros_like(east)
    for copy in copies:
        copy.wait()

    def load(slot, d):
        other = table[me, d]
        place = jnp.where(other == count, 0, lax.rem(me - other + count, count))
        strips[slot] = slots[place].astype(jnp.float32)

    for edge, (left, centre, right) in ((top, (4, 0, 5)), (bottom, (6, 1, 7))):
        load(0, left)
        load(1, centre)
        load(2, right)
        for k in range(3):
            edge[k, 5:8] = strips[0, k * side + side - 3 : k * side + side]
            edge[k, 8 : 8 + side] = strips[1, k * side : k * side + side]
            edge[k, 8 + side : 11 + side] = strips[2, k * side : k * side + 3]
    load(0, 2)
    load(1, 3)
    for h in range(side):
        west[h, 5:8] = strips[0, 3 * h : 3 * h + 3]
        east[h, 0:3] = strips[1, 3 * h : 3 * h + 3]
    if rest:
        part_out[...] = part[far].astype(jnp.float32)
        for i, copy in enumerate(far_copies):
            copy.wait()
            part_out[...] += part_recv[i].astype(jnp.float32)


def exchange_rims(tile, table, count, call, part=None):
    side, _, channels = tile.shape
    vmem = pl.BlockSpec(memory_space=pltpu.VMEM)
    edge = jax.ShapeDtypeStruct((3, side + 16, channels), jnp.float32)
    flank = jax.ShapeDtypeStruct((side, 8, channels), jnp.float32)
    rest, outs, more, operands = 0, (edge, edge, flank, flank), [], [table, tile]
    if part is not None:
        rest = part.shape[0]
        outs += (jax.ShapeDtypeStruct(part.shape[1:], jnp.float32),)
        more = [
            pltpu.VMEM((rest - 1,) + part.shape[1:], part.dtype),
            pltpu.SemaphoreType.DMA((2, rest - 1)),
        ]
        operands.append(part)
    return pl.pallas_call(
        functools.partial(rim_body, count, rest),
        out_shape=outs,
        in_specs=[pl.BlockSpec(memory_space=pltpu.SMEM)] + [vmem] * (len(operands) - 1),
        out_specs=(vmem,) * len(outs),
        scratch_shapes=[
            pltpu.VMEM((4, 3 * side, channels), jnp.float32),
            pltpu.VMEM((count - 1, 3 * side, channels), jnp.bfloat16),
            pltpu.VMEM((count, 3 * side, channels), jnp.bfloat16),
            pltpu.SemaphoreType.DMA((count - 1,)),
            pltpu.SemaphoreType.DMA((count - 1,)),
            *more,
        ],
        compiler_params=params(collective_id=call, has_side_effects=True),
        cost_estimate=pl.CostEstimate(
            flops=10**10, bytes_accessed=8 << 20, transcendentals=0
        ),
        name="rims" + str(call),
    )(*operands)


def fill(ext, tile_ref, top_ref, bottom_ref, west_ref, east_ref):
    side = tile_ref.shape[0]
    ext[0:3] = top_ref[...]
    ext[side + 3 : side + 6] = bottom_ref[...]
    ext[3 : side + 3, 0:8] = west_ref[...]
    ext[3 : side + 3, 8 : side + 8] = tile_ref[...].astype(jnp.float32)
    ext[3 : side + 3, side + 8 : side + 16] = east_ref[...]


def conv_body(tile_ref, top, bottom, west, east, weight_ref, out_ref, ext, shifted, total):
    conv_sum(tile_ref, top, bottom, west, east, weight_ref, ext, shifted, total)
    out_ref[...] = total[...]


def conv_sum(
    tile_ref, top, bottom, west, east, weight_ref, ext, shifted, total, flipped=False
):
    side = tile_ref.shape[0]
    fill(ext, tile_ref, top, bottom, west, east)
    for b in range(7):
        if b == 3:
            source, base = ext, 8
        else:
            shifted[...] = ext[:, 5 + b : 5 + b + side]
            source, base = shifted, 0
        spots = [48 - a * 7 - b if flipped else a * 7 + b for a in range(7)]
        taps = [jnp.broadcast_to(weight_ref[at : at + 1, :], (8, lanes)) for at in spots]

        def rows(step, carry, b=b, source=source, base=base, taps=taps):
            first = step * row_step
            for group in range(side // 8):
                at = pl.ds(base + group * 8, 8)
                here = pl.ds(group * 8, 8)
                sums = [None] * row_step
                for r in range(row_step + 6):
                    value = source[first + r, at]
                    for i in range(row_step):
                        a = r - i
                        if 0 <= a < 7:
                            term = value * taps[a]
                            sums[i] = term if sums[i] is None else sums[i] + term
                for i in range(row_step):
                    if b > 0:
                        sums[i] = sums[i] + total[first + i, here]
                    total[first + i, here] = sums[i]
            return carry

        lax.fori_loop(0, side // row_step, rows, 0)


def back_body(
    extents,
    tile_ref,
    top,
    bottom,
    west,
    east,
    weight_ref,
    add_ref,
    down,
    small,
    out_ref,
    down_out,
    small_out,
    ext,
    shifted,
    total,
    down_recv,
    small_recv,
    slide_slots,
    tile_slots,
    down_sems,
    small_sems,
    slide_sems,
    tile_sems,
):
    slides, tiles = extents
    rest = slides // 2
    step = pl.program_id(0)
    slide, tile = lax.axis_index("slide"), lax.axis_index("tile")
    far, core = slide // 2, lax.rem(slide, 2)
    next_tile = [lax.rem(tile + o, tiles) for o in range(1, tiles)]
    next_slide = [lax.rem(slide + o, slides) for o in range(1, slides)]
    next_far = [lax.rem(far + o, rest) for o in range(1, rest)]

    def remote(source, target, sems, i, device):
        return pltpu.make_async_remote_copy(
            src_ref=source,
            dst_ref=target,
            send_sem=sems.at[0, i],
            recv_sem=sems.at[1, i],
            device_id=device,
            device_id_type=pl.DeviceIdType.MESH,
        )

    def far_copies(part, recv, sems):
        return [
            remote(part.at[at], recv.at[i], sems, i, {"slide": at * 2 + core})
            for i, at in enumerate(next_far)
        ]

    def small_copies():
        return [
            remote(small.at[at], small_recv.at[i], small_sems, i, {"tile": at})
            for i, at in enumerate(next_tile)
        ]

    def slide_copies():
        return [
            remote(slide_slots.at[0], slide_slots.at[i + 1], slide_sems, i, {"slide": at})
            for i, at in enumerate(next_slide)
        ]

    def tile_copies():
        return [
            remote(tile_slots.at[0], tile_slots.at[i + 1], tile_sems, i, {"tile": at})
            for i, at in enumerate(next_tile)
        ]

    @pl.when(step == 0)
    def _():
        barrier = pltpu.get_barrier_semaphore()
        peers = [{"tile": at} for at in next_tile] + [{"slide": at} for at in next_slide]
        for peer in peers:
            pl.semaphore_signal(
                barrier, inc=1, device_id=peer, device_id_type=pl.DeviceIdType.MESH
            )
        pl.semaphore_wait(barrier, len(peers))
        for copy in small_copies():
            copy.start()

    @pl.when(step == 1)
    def _():
        own = small[tile]
        for i, copy in enumerate(small_copies()):
            copy.wait()
            own = own + small_recv[i]
        slide_slots[0] = own
        for copy in slide_copies() + far_copies(down, down_recv, down_sems):
            copy.start()

    @pl.when(step == 4)
    def _():
        for copy in slide_copies():
            copy.wait()
        own = slide_slots[lax.rem(slide, slides)]
        for i in range(1, slides):
            own = own + slide_slots[lax.rem(slide - i + slides, slides)]
        tile_slots[0] = own
        for copy in tile_copies():
            copy.start()

    conv_sum(tile_ref, top, bottom, west, east, weight_ref, ext, shifted, total, True)
    out_ref[...] = (add_ref[...].astype(jnp.float32) + total[...]).astype(jnp.bfloat16)

    @pl.when(step == pl.num_programs(0) - 1)
    def _():
        for copy in tile_copies():
            copy.wait()
        for i in range(tiles):
            small_out[i] = tile_slots[lax.rem(tile - i + tiles, tiles)]
        down_out[...] = down[far].astype(jnp.float32)
        for i, copy in enumerate(far_copies(down, down_recv, down_sems)):
            copy.wait()
            down_out[...] += down_recv[i].astype(jnp.float32)


def depthwise_and_sums(tile, rims, weight, add, down, small, slides, tiles):
    side, _, channels = tile.shape
    rest, rows = down.shape[0], down.shape[1]
    chunk = small.shape[1]
    operands = [tile, *rims, weight, add]
    fixed = lambda shape: pl.BlockSpec(
        shape, lambda c: (0,) * len(shape), pipeline_mode=pl.Buffered(buffer_count=1)
    )
    shape = jax.ShapeDtypeStruct
    wide, narrow = jnp.float32, jnp.bfloat16
    return pl.pallas_call(
        functools.partial(back_body, (slides, tiles)),
        out_shape=(
            shape(tile.shape, narrow),
            shape((rows, channels), wide),
            shape(small.shape, wide),
        ),
        grid=(channels // lanes,),
        in_specs=[tile_spec(o.shape) for o in operands]
        + [fixed(down.shape), fixed(small.shape)],
        out_specs=(
            tile_spec(tile.shape),
            fixed((rows, channels)),
            fixed(small.shape),
        ),
        scratch_shapes=[
            pltpu.VMEM((side + 6, side + 16, lanes), wide),
            pltpu.VMEM((side + 6, side, lanes), wide),
            pltpu.VMEM((side, side, lanes), wide),
            pltpu.VMEM((rest - 1, rows, channels), narrow),
            pltpu.VMEM((tiles - 1, chunk, channels), wide),
            pltpu.VMEM((slides, chunk, channels), wide),
            pltpu.VMEM((tiles, chunk, channels), wide),
            pltpu.SemaphoreType.DMA((2, rest - 1)),
            pltpu.SemaphoreType.DMA((2, tiles - 1)),
            pltpu.SemaphoreType.DMA((2, slides - 1)),
            pltpu.SemaphoreType.DMA((2, tiles - 1)),
        ],
        compiler_params=params(collective_id=3, has_side_effects=True),
        cost_estimate=pl.CostEstimate(
            flops=2 * 10**10, bytes_accessed=8 << 20, transcendentals=0
        ),
        name="depthwise_and_sums",
    )(*operands, down, small)


def tile_spec(shape):
    return pl.BlockSpec(shape[:-1] + (lanes,), lambda c: (0,) * (len(shape) - 1) + (c,))


def depthwise(tile, rims, weight):
    side, _, channels = tile.shape
    operands = [tile, *rims, weight]
    flops = 2 * 49 * side * side * channels
    return pl.pallas_call(
        conv_body,
        out_shape=jax.ShapeDtypeStruct(tile.shape, jnp.float32),
        grid=(channels // lanes,),
        in_specs=[tile_spec(o.shape) for o in operands],
        out_specs=tile_spec(tile.shape),
        scratch_shapes=[
            pltpu.VMEM((side + 6, side + 16, lanes), jnp.float32),
            pltpu.VMEM((side + 6, side, lanes), jnp.float32),
            pltpu.VMEM((side, side, lanes), jnp.float32),
        ],
        compiler_params=params(),
        cost_estimate=pl.CostEstimate(flops=260 * flops, bytes_accessed=8 << 20, transcendentals=0),
        name="depthwise",
    )(*operands)


def kernel_grad_body(tile_ref, top, bottom, west, east, grad_ref, out_ref, ext, shifted, grad):
    side = tile_ref.shape[0]
    fill(ext, tile_ref, top, bottom, west, east)
    grad[...] = grad_ref[...].astype(jnp.float32)
    for b in range(7):
        if b == 3:
            source, base = ext, 8
        else:
            shifted[...] = ext[:, 5 + b : 5 + b + side]
            source, base = shifted, 0

        def rows(step, sums, source=source, base=base):
            first = step * row_step
            sums = list(sums)
            for group in range(side // 8):
                at = pl.ds(base + group * 8, 8)
                here = pl.ds(group * 8, 8)
                near = [grad[first + i, here] for i in range(row_step)]
                for r in range(row_step + 6):
                    value = source[first + r, at]
                    for i in range(row_step):
                        a = r - i
                        if 0 <= a < 7:
                            slot = a * 2 + i % 2
                            sums[slot] = sums[slot] + value * near[i]
            return tuple(sums)

        zero = jnp.zeros((8, lanes), jnp.float32)
        sums = lax.fori_loop(0, side // row_step, rows, (zero,) * 14)
        for a in range(7):
            out_ref[a * 7 + b : a * 7 + b + 1, :] = jnp.sum(
                sums[2 * a] + sums[2 * a + 1], axis=0, keepdims=True
            )


def kernel_grad(tile, rims, conv_grad):
    side, _, channels = tile.shape
    operands = [tile, *rims, conv_grad]
    flops = 2 * 49 * side * side * channels
    return pl.pallas_call(
        kernel_grad_body,
        out_shape=jax.ShapeDtypeStruct((49, channels), jnp.float32),
        grid=(channels // lanes,),
        in_specs=[tile_spec(o.shape) for o in operands],
        out_specs=tile_spec((49, channels)),
        scratch_shapes=[
            pltpu.VMEM((side + 6, side + 16, lanes), jnp.float32),
            pltpu.VMEM((side + 6, side, lanes), jnp.float32),
            pltpu.VMEM((side, side, lanes), jnp.float32),
        ],
        compiler_params=params(),
        cost_estimate=pl.CostEstimate(flops=260 * flops, bytes_accessed=8 << 20, transcendentals=0),
        name="kernel_grad",
    )(*operands)


def nt(left, right):
    return lax.dot_general(
        left, right, (((1,), (1,)), ((), ())), preferred_element_type=jnp.float32
    )


def nn(left, right):
    return jnp.dot(left, right, preferred_element_type=jnp.float32)


def mlp_body(
    extents,
    conv_ref,
    x_ref,
    g_ref,
    keep_ref,
    gain_ref,
    shift_ref,
    up_ref,
    up_bias_ref,
    down_ref,
    down_bias_ref,
    scale_ref,
    block_out_ref,
    conv_grad_ref,
    up_grad_ref,
    down_grad_ref,
    sums_ref,
    bias_ref,
    flat,
    branch_grad,
    inv,
    white,
    branch,
    normed_grad,
    core_send,
    core_recv,
    up_sum,
    down_sum,
    up_recv,
    down_recv,
    core_sems,
    up_sems,
    down_sems,
):
    step = pl.program_id(0)
    pixels, channels = conv_ref.shape
    part = 128
    rest, his, los = extents
    slide, tile = lax.axis_index("slide"), lax.axis_index("tile")
    core, hi, lo = lax.rem(slide, 2), tile // los, lax.rem(tile, los)
    rows = core_send.shape[1] // (his * los)
    core_peer = {"slide": slide + 1 - 2 * core}
    hi_peer = {"tile": (1 - hi) * los + lo}
    lo_next = [lax.rem(lo + offset, los) for offset in range(1, los)]
    lo_peers = [{"tile": hi * los + other} for other in lo_next]

    def remote(source, target, sems, device):
        return pltpu.make_async_remote_copy(
            src_ref=source,
            dst_ref=target,
            send_sem=sems[0],
            recv_sem=sems[1],
            device_id=device,
            device_id_type=pl.DeviceIdType.MESH,
        )

    def core_copy(b):
        sems = (core_sems.at[0, b], core_sems.at[1, b])
        return remote(core_send.at[b], core_recv.at[b], sems, core_peer)

    def up_copy(b):
        sems = (up_sems.at[0, b], up_sems.at[1, b])
        return remote(up_sum.at[b, 1 - hi], up_recv.at[b], sems, hi_peer)

    def down_copy(b, i):
        sems = (down_sems.at[0, b, i], down_sems.at[1, b, i])
        return remote(down_sum.at[b, lo_next[i]], down_recv.at[b, i], sems, lo_peers[i])

    @pl.when(step == 0)
    def _():
        barrier = pltpu.get_barrier_semaphore()
        peers = [core_peer, hi_peer] + lo_peers
        for peer in peers:
            pl.semaphore_signal(
                barrier, inc=1, device_id=peer, device_id_type=pl.DeviceIdType.MESH
            )
        pl.semaphore_wait(barrier, len(peers))

    @pl.when(step == 0)
    def _():
        keep = keep_ref[0:1, 0:1]

        def body(i, total):
            at = pl.ds(pl.multiple_of(i * part, part), part)
            values = conv_ref[at, :]
            centred = values - jnp.mean(values, axis=-1, keepdims=True)
            inv_std = lax.rsqrt(jnp.mean(centred * centred, axis=-1, keepdims=True) + ln_eps)
            whitened = centred * inv_std
            white[at, :] = whitened
            inv[at, :] = jnp.broadcast_to(inv_std, (part, lanes))
            flat[at, :] = (whitened * gain_ref[...] + shift_ref[...]).astype(jnp.bfloat16)
            own = (keep * scale_ref[...] * g_ref[at, :].astype(jnp.float32)).astype(jnp.bfloat16)
            branch_grad[at, :] = own
            return total + jnp.sum(own.astype(jnp.float32), axis=0, keepdims=True)

        zero = jnp.zeros((1, channels), jnp.float32)
        sums_ref[2:3, :] = lax.fori_loop(0, pixels // part, body, zero)
        branch[...] = jnp.zeros_like(branch)
        normed_grad[...] = jnp.zeros_like(normed_grad)

    up = up_ref[...]
    down = down_ref[0] if len(down_ref.shape) == 3 else down_ref[...]
    pre = nt(flat[...], up) + up_bias_ref[0]
    act_grad = nn(branch_grad[...], down)
    cdf = 0.5 * (1.0 + lax.erf(pre * root_half))
    slope = cdf + pre * inv_root_two_pi * jnp.exp(-0.5 * pre * pre)
    act = (pre * cdf).astype(jnp.bfloat16)
    pre_grad_wide = act_grad * slope
    pre_grad = pre_grad_wide.astype(jnp.bfloat16)
    branch[...] += nt(act, down)
    normed_grad[...] += nn(pre_grad, up)
    bias_ref[0] = jnp.sum(pre_grad.astype(jnp.float32), axis=0, keepdims=True)
    up_grad = nn(pre_grad.T, flat[...])
    down_grad = nn(act.T, branch_grad[...])

    @pl.when(step < rest)
    def _():
        core_send[step, :, 0:channels] = up_grad.astype(jnp.bfloat16)
        core_send[step, :, channels : 2 * channels] = down_grad.astype(jnp.bfloat16)
        core_copy(step).start()

    @pl.when(step >= rest)
    def _():
        b = step - rest
        core_copy(b).wait_recv()
        up_total = up_grad + core_recv[b, :, 0:channels].astype(jnp.float32)
        down_total = down_grad + core_recv[b, :, channels : 2 * channels].astype(jnp.float32)
        for h in range(his):
            for l in range(los):
                at = (h * los + l) * rows
                up_sum[b, h, l] = up_total[at : at + rows].astype(jnp.bfloat16)
                down_sum[b, l, h] = down_total[at : at + rows].astype(jnp.bfloat16)
        up_copy(b).start()
        for i in range(los - 1):
            down_copy(b, i).start()

    @pl.when(step == pl.num_programs(0) - 1)
    def _():
        keep = keep_ref[0:1, 0:1]

        def body(i, totals):
            at = pl.ds(pl.multiple_of(i * part, part), part)
            out = branch[at, :] + down_bias_ref[...]
            g = g_ref[at, :].astype(jnp.float32)
            block_out_ref[at, :] = (
                x_ref[at, :].astype(jnp.float32) + keep * scale_ref[...] * out
            ).astype(jnp.bfloat16)
            whitened = white[at, :]
            own = normed_grad[at, :]
            scaled = own * gain_ref[...]
            spread = whitened * jnp.mean(scaled * whitened, axis=-1, keepdims=True)
            centred = scaled - jnp.mean(scaled, axis=-1, keepdims=True) - spread
            conv_grad_ref[at, :] = (inv[at, 0:1] * centred).astype(jnp.bfloat16)
            down_sum = lambda v: jnp.sum(v, axis=0, keepdims=True)
            terms = (own * whitened, own, g * keep * out)
            return tuple(t + down_sum(v) for t, v in zip(totals, terms))

        zero = jnp.zeros((1, channels), jnp.float32)
        totals = lax.fori_loop(0, pixels // part, body, (zero,) * 3)
        sums_ref[0:1, :] = totals[0]
        sums_ref[1:2, :] = totals[1]
        sums_ref[3:4, :] = totals[2]

        def finish(b, carry):
            core_copy(b).wait_send()
            up_copy(b).wait()
            total = up_sum[b, hi].astype(jnp.float32) + up_recv[b].astype(jnp.float32)
            up_grad_ref[b] = total.astype(jnp.bfloat16)
            total = down_sum[b, lo].astype(jnp.float32)
            for i in range(los - 1):
                down_copy(b, i).wait()
                total = total + down_recv[b, i].astype(jnp.float32)
            down_grad_ref[b] = total.astype(jnp.bfloat16)
            return carry

        lax.fori_loop(0, rest, finish, 0)


def mlp(conv, x, g, keep, gain, shift, up, up_bias, down, down_bias, scale, slides, tiles):
    pixels, channels = conv.shape
    hidden = up.shape[0]
    rest, his, los = slides // 2, 2, tiles // 2
    blocks = 2 * rest
    block = hidden // blocks
    rows = block // tiles
    single = pl.Buffered(buffer_count=1)
    whole = lambda shape: pl.BlockSpec(
        shape, lambda j: (0,) * len(shape), pipeline_mode=single
    )
    row = pl.BlockSpec((1, channels), lambda j: (0, 0))

    def at(j):
        core = lax.rem(lax.axis_index("slide"), 2)
        return lax.rem(j, rest) * 2 + jnp.where(j < rest, 1 - core, core)

    if block % lanes == 0:
        down_spec = pl.BlockSpec((channels, block), lambda j: (0, at(j)))
    else:
        down = jnp.transpose(down.reshape(channels, blocks, block), (1, 0, 2))
        down_spec = pl.BlockSpec((1, channels, block), lambda j: (at(j), 0, 0))
    bias_spec = pl.BlockSpec((1, 1, block), lambda j: (at(j), 0, 0))
    shape = jax.ShapeDtypeStruct
    wide, narrow = jnp.float32, jnp.bfloat16
    return pl.pallas_call(
        functools.partial(mlp_body, (rest, his, los)),
        out_shape=(
            shape((pixels, channels), narrow),
            shape((pixels, channels), narrow),
            shape((rest, los, rows, channels), narrow),
            shape((rest, his, rows, channels), narrow),
            shape((4, channels), wide),
            shape((blocks, 1, block), wide),
        ),
        grid=(blocks,),
        in_specs=[
            whole((pixels, channels)),
            whole((pixels, channels)),
            whole((pixels, channels)),
            pl.BlockSpec((1, lanes), lambda j: (0, 0)),
            row,
            row,
            pl.BlockSpec((block, channels), lambda j: (at(j), 0)),
            bias_spec,
            down_spec,
            row,
            row,
        ],
        out_specs=(
            whole((pixels, channels)),
            whole((pixels, channels)),
            whole((rest, los, rows, channels)),
            whole((rest, his, rows, channels)),
            pl.BlockSpec((4, channels), lambda j: (0, 0)),
            bias_spec,
        ),
        scratch_shapes=[
            pltpu.VMEM((pixels, channels), narrow),
            pltpu.VMEM((pixels, channels), narrow),
            pltpu.VMEM((pixels, lanes), wide),
            pltpu.VMEM((pixels, channels), wide),
            pltpu.VMEM((pixels, channels), wide),
            pltpu.VMEM((pixels, channels), wide),
            pltpu.VMEM((rest, block, 2 * channels), narrow),
            pltpu.VMEM((rest, block, 2 * channels), narrow),
            pltpu.VMEM((rest, his, los, rows, channels), narrow),
            pltpu.VMEM((rest, los, his, rows, channels), narrow),
            pltpu.VMEM((rest, los, rows, channels), narrow),
            pltpu.VMEM((rest, los - 1, his, rows, channels), narrow),
            pltpu.SemaphoreType.DMA((2, rest)),
            pltpu.SemaphoreType.DMA((2, rest)),
            pltpu.SemaphoreType.DMA((2, rest, los - 1)),
        ],
        compiler_params=params(collective_id=2, has_side_effects=True),
        cost_estimate=pl.CostEstimate(
            flops=12 * pixels * channels * hidden,
            bytes_accessed=32 << 20,
            transcendentals=2 * pixels * hidden,
        ),
        name="mlp",
    )(conv, x, g, keep, gain, shift, up, up_bias.reshape(blocks, 1, block), down, down_bias, scale)


class Grid:
    def __init__(self, slides, tiles):
        self.sizes = {"rest": slides // 2, "core": 2, "hi": 2, "lo": tiles // 2}
        self.names = ("rest", "core", "hi", "lo")
        slide, tile = lax.axis_index("slide"), lax.axis_index("tile")
        self.place = {
            "rest": slide // 2,
            "core": lax.rem(slide, 2),
            "hi": tile // (tiles // 2),
            "lo": lax.rem(tile, tiles // 2),
        }

    def perm(self, axis, move):
        pairs = []
        extents = [self.sizes[n] for n in self.names]
        at = self.names.index(axis)
        stride = 1
        for size in extents[at + 1 :]:
            stride *= size
        total = 1
        for size in extents:
            total *= size
        for device in range(total):
            own = (device // stride) % extents[at]
            pairs.append((device, device + (move(own) - own) * stride))
        return pairs

    def send(self, value, axis, move):
        return lax.ppermute(value, ("slide", "tile"), self.perm(axis, move))

    def scatter(self, value, dim, axis, last=False):
        size, own = self.sizes[axis], self.place[axis]
        pick = lambda i: lax.dynamic_index_in_dim(value, i, dim, keepdims=False)
        total = pick(own).astype(jnp.float32)
        for offset in range(1, size):
            block = pick(lax.rem(own + offset, size))
            came = self.send(block, axis, lambda i, o=offset: (i + o) % size)
            total = total + came.astype(jnp.float32)
        return total if last else total.astype(jnp.bfloat16)


def on_device(
    features,
    cotangent,
    neighbours,
    skip_flags,
    dw_weight,
    ln_gain,
    ln_bias,
    up_weight,
    up_bias,
    down_weight,
    down_bias,
    layer_scale,
):
    slides, tiles = lax.axis_size("slide"), lax.axis_size("tile")
    side, channels = features.shape[3], features.shape[4]
    hidden = up_weight.shape[1]
    table = neighbours[0]
    grid = Grid(slides, tiles)
    tile, grad = features[0, 0], cotangent[0, 0]
    taps = dw_weight[0].reshape(49, channels)
    keep = jnp.broadcast_to((1 - skip_flags[0, 0]).astype(jnp.float32), (1, lanes))

    rims = exchange_rims(tile, table, tiles, 0)
    conv = depthwise(tile, rims, taps)
    block_out, conv_grad, up_grad, down_grad, sums, bias = mlp(
        conv.reshape(-1, channels),
        tile.reshape(-1, channels),
        grad.reshape(-1, channels),
        keep,
        ln_gain,
        ln_bias,
        up_weight[0],
        up_bias,
        down_weight[0],
        down_bias,
        layer_scale,
        slides,
        tiles,
    )
    conv_tile = conv_grad.reshape(side, side, channels)
    kernel_sum = kernel_grad(tile, rims, conv_tile)
    up_part = grid.scatter(up_grad, 1, "lo")
    down_part = grid.scatter(down_grad, 1, "hi")
    conv_tile, kernel_sum, up_part, down_part = lax.optimization_barrier(
        (conv_tile, kernel_sum, up_part, down_part)
    )
    small = jnp.concatenate([kernel_sum, sums, bias.reshape(-1, channels)], 0)
    count = small.shape[0]
    small = jnp.pad(small, ((0, -count % (8 * tiles)), (0, 0))).reshape(tiles, -1, channels)
    *grad_rims, up_part = exchange_rims(conv_tile, table, tiles, 1, up_part)
    input_grad, down_part, small = depthwise_and_sums(
        conv_tile, grad_rims, taps, grad, down_part, small, slides, tiles
    )
    small = small.reshape(-1, channels)
    weight_grads = jnp.concatenate([up_part, down_part], -1)[None]
    return (
        block_out.reshape(1, 1, side, side, channels),
        input_grad[None, None],
        weight_grads,
        small[:49].reshape(1, 7, 7, channels),
        small[49:53][None],
        small[53:count].reshape(1, hidden),
    )


def solution(mesh):
    tiles = P("slide", "tile", None, None, None)
    return jax.shard_map(
        on_device,
        mesh=mesh,
        in_specs=(tiles, tiles, P("slide", None, None), P(None, "slide")) + (P(),) * 8,
        out_specs=(tiles, tiles, P(None, ("slide", "tile"), None), P(), P(), P()),
        check_vma=False,
    )
```
